128 devices in a mesh: band: 16 (over x, z_lo, core), pair: 8 (over y, z_hi).
Axes of the slice: x: 4, y: 4, z: 4 (z_hi: 2, z_lo: 2; z = z_hi * 2 + z_lo), core: 2. Of those that a mesh axis runs over, the one named last changes fastest.
Arguments:
- orbitals: float32 [96, 64, 64, 128], P('band'), may hold values from -0.8 to 0.8
Outputs:
- exchange_terms: float32 [96, 64, 64, 128], P('band', 'pair')
The draws below stay inside these ranges and needn't reach their ends.
All inputs are finite; a program needn't handle non-finite values.
Results may differ from the reference program's by a relative error of at most 0.0003.
Values sent between devices are 32-bit elements; how exact they have to be, the bound alone decides.
A program may use at most 128 MiB of HBM per device.

```python
import math
import jax
import jax.numpy as jnp
import numpy as np
from jax import lax

GX = 64
GY = 64
GZ = 128
ORB_DEV = 6
NORB = 96
N_BAND = 16


def draw_orbitals(key, part):
    key = jax.random.fold_in(key, 7)
    offset_key, noise_key = jax.random.split(key, 2)
    offset = jax.random.uniform(offset_key, (NORB, 1, 1, 1), jnp.float32, 0.3, 0.8)
    noise = jnp.clip(jax.random.normal(noise_key, (NORB, GX, GY, GZ), jnp.float32), -5.0, 5.0)
    return 0.1 * (offset + noise)


def setup_inputs(seed: int = 0) -> dict:
    key_of = jax.random.split(jax.random.key(seed), 2)
    orbitals = draw_orbitals(jax.random.fold_in(key_of[1], 71), 0)
    return dict(orbitals=orbitals)


grid_spacing = 0.6
screening = 0.106


def signed_freq(count):
    steps = jnp.arange(count, dtype=jnp.int32)
    signed = jnp.where(steps <= count // 2, steps, steps - count)
    return signed.astype(jnp.float32) * (2.0 * math.pi / (count * grid_spacing))


def screened_kernel(size_x, size_y, size_z):
    fx = signed_freq(size_x)
    fy = signed_freq(size_y)
    fz = signed_freq(size_z)
    square = fx[:, None, None] ** 2 + fy[None, :, None] ** 2 + fz[None, None, :] ** 2
    safe = jnp.where(square > 0, square, jnp.ones_like(square))
    value = 4.0 * math.pi / safe * (-jnp.expm1(-safe / (4.0 * screening * screening)))
    return jnp.where(square > 0, value, jnp.full_like(value, math.pi / (screening * screening)))


def pair_list(count):
    listed = [(first, second, 0) for first in range(count) for second in range(first, count)]
    listed += [(first, second, 1) for first in range(count) for second in range(count)]
    return np.array(listed, dtype=np.int32)


def poisson(density, kernel):
    spectrum = jnp.fft.fftn(density) * kernel
    return jnp.real(jnp.fft.ifftn(spectrum)).astype(density.dtype)


def reference(orbitals):
    kernel = screened_kernel(GX, GY, GZ)
    pairs = jnp.asarray(pair_list(ORB_DEV))

    def block_terms(block):
        start = (block * ORB_DEV).astype(jnp.int32)
        after = (((block + 1) % N_BAND) * ORB_DEV).astype(jnp.int32)
        local_block = lax.dynamic_slice_in_dim(orbitals, start, ORB_DEV, 0)
        partner = lax.dynamic_slice_in_dim(orbitals, after, ORB_DEV, 0)

        def step(carry, entries):
            local_terms, next_terms = carry
            first, second, kind = entries[0], entries[1], entries[2]
            orbital_a = lax.dynamic_index_in_dim(local_block, first, 0, keepdims=False)
            orbital_b = jnp.where(kind == 1,
                                  lax.dynamic_index_in_dim(partner, second, 0, keepdims=False),
                                  lax.dynamic_index_in_dim(local_block, second, 0, keepdims=False))
            potential = poisson(orbital_a * orbital_b, kernel)
            local_terms = local_terms.at[first].add(-orbital_b * potential)
            mirrored = -orbital_a * potential
            same_flag = jnp.logical_and(kind == 0, first != second).astype(orbitals.dtype)
            cycle_flag = (kind == 1).astype(orbitals.dtype)
            local_terms = local_terms.at[second].add(same_flag * mirrored)
            next_terms = next_terms.at[second].add(cycle_flag * mirrored)
            return (local_terms, next_terms), None

        empty = jnp.zeros_like(local_block)
        (local_terms, next_terms), _ = lax.scan(step, (empty, empty), pairs)
        return local_terms, next_terms

    local_all, next_all = lax.map(block_terms, jnp.arange(N_BAND, dtype=jnp.int32))
    total = local_all + jnp.roll(next_all, 1, axis=0)
    return total.reshape(NORB, GX, GY, GZ)
```

```python
import functools
import math

import jax
import jax.numpy as jnp
import ml_dtypes
import numpy as np
from jax import lax
from jax.experimental import pallas as pl
from jax.experimental.pallas import tpu as pltpu
from jax.sharding import PartitionSpec as P

grid_spacing = 0.6
screening = 0.106

f32 = jnp.float32
bf16 = jnp.bfloat16
N_BAND = 16
N_PAIR = 8
NX = 64
NY = 64
NZ = 128
ROWS = NX * NY
VMEM_LIMIT = 56 * 2**20


def signed_freq(count):
    steps = jnp.arange(count, dtype=jnp.int32)
    signed = jnp.where(steps <= count // 2, steps, steps - count)
    return signed.astype(jnp.float32) * (2.0 * math.pi / (count * grid_spacing))


def screened_kernel():
    fx = signed_freq(NX)
    fy = signed_freq(NY)
    fz = signed_freq(NZ)
    square = fy[:, None, None] ** 2 + fx[None, :, None] ** 2 + fz[None, None, :] ** 2
    safe = jnp.where(square > 0, square, jnp.ones_like(square))
    value = 4.0 * math.pi / safe * -jnp.expm1(-safe / (4.0 * screening * screening))
    value = jnp.where(square > 0, value, jnp.full_like(value, math.pi / (screening * screening)))
    return (value * (-1.0 / (NX * NY * NZ))).reshape(ROWS, NZ)


def cas(count):
    k = np.arange(count)
    angles = 2.0 * np.pi * ((k[:, None] * k[None, :]) % count) / count
    return np.cos(angles) + np.sin(angles)


def split_table(table):
    high = table.astype(ml_dtypes.bfloat16)
    low = (table - high.astype(np.float64)).astype(ml_dtypes.bfloat16)
    return high, low


def tables():
    high, low = split_table(cas(NZ))
    along_z = np.block([[high, low], [high, low]])
    high, low = split_table(cas(NY))
    zero = np.zeros_like(high)
    high = np.block([[high, zero], [zero, high]])
    low = np.block([[low, zero], [zero, low]])
    along_rows = np.block([[high, high], [low, low]])
    return jnp.asarray(along_z), jnp.asarray(along_rows)


def split(value):
    high = value.astype(bf16)
    low = (value - high.astype(f32)).astype(bf16)
    return high, low


def lanes_stage(value, table):
    high, low = split(value)
    out = jnp.dot(jnp.concatenate([high, low], axis=1), table, preferred_element_type=f32)
    return out[:, :NZ] + out[:, NZ:]


def rows_stage(tile, table):
    high, low = split(tile)
    out = jnp.dot(table, jnp.concatenate([high, low], axis=0), preferred_element_type=f32)
    return out[:128] + out[128:]


def to_tile(value):
    return jnp.concatenate([value[:128], value[128:]], axis=1)


def from_tile(tile):
    return jnp.concatenate([tile[:, :128], tile[:, 128:]], axis=0)


def forward(load, table_z, table_r, first_ref):
    def step(i, _):
        rows = pl.ds(pl.multiple_of(i * 256, 256), 256)
        value = lanes_stage(load(rows), table_z)
        first_ref[rows, :] = from_tile(rows_stage(to_tile(value), table_r))
        return 0

    lax.fori_loop(0, 16, step, 0, unroll=16)


def middle(kernel_ref, table_r, first_ref, second_ref):
    def step(i, _):
        c = [first_ref[pl.ds(i * 4 + q, 64, stride=64), :] for q in range(4)]
        left = jnp.concatenate([c[0], c[1]], axis=0)
        right = jnp.concatenate([c[2], c[3]], axis=0)
        tile = rows_stage(jnp.concatenate([left, right], axis=1), table_r)
        rows = pl.ds(pl.multiple_of(i * 256, 256), 256)
        tile = tile * to_tile(kernel_ref[rows, :])
        value = from_tile(rows_stage(tile, table_r))
        for q in range(4):
            second_ref[pl.ds(i * 4 + q, 64, stride=64), :] = value[q * 64 : (q + 1) * 64]
        return 0

    lax.fori_loop(0, 16, step, 0, unroll=16)


def backward(emit, table_z, table_r, second_ref):
    def step(i, _):
        rows = pl.ds(pl.multiple_of(i * 256, 256), 256)
        tile = rows_stage(to_tile(second_ref[rows, :]), table_r)
        emit(i, rows, lanes_stage(from_tile(tile), table_z))
        return 0

    lax.fori_loop(0, 16, step, 0, unroll=16)


def near_kernel(
    plan_ref, a_ref, b_ref, other_ref, kernel_ref, z_ref, r_ref, sum_ref, first_ref, second_ref
):
    step = pl.program_id(0)
    table_z, table_r = z_ref[...], r_ref[...]

    @pl.when(step == 0)
    def _():
        sum_ref[...] = jnp.zeros_like(sum_ref)

    @pl.when(plan_ref[2, step] == 1)
    def _():
        own = step < 4
        mine = plan_ref[3, step]

        def partner(rows):
            return jnp.where(own, b_ref[rows, :], other_ref[rows, :])

        forward(lambda rows: a_ref[rows, :] * partner(rows), table_z, table_r, first_ref)
        middle(kernel_ref, table_r, first_ref, second_ref)

        @pl.when(step == 0)
        def _():
            weight = plan_ref[5, 0].astype(f32)
            mirror = plan_ref[4, 0]

            def emit(i, rows, value):
                sum_ref[mine, rows, :] += b_ref[rows, :] * value
                sum_ref[mirror, rows, :] += weight * a_ref[rows, :] * value

            backward(emit, table_z, table_r, second_ref)

        @pl.when(step > 0)
        def _():
            def emit(i, rows, value):
                sum_ref[mine, rows, :] += partner(rows) * value

            backward(emit, table_z, table_r, second_ref)


def far_kernel(
    plan_ref, a_ref, one_ref, two_ref, kernel_ref, z_ref, r_ref, part_ref, out_ref, first_ref, second_ref
):
    step = pl.program_id(0)
    table_z, table_r = z_ref[...], r_ref[...]
    shift = plan_ref[1]

    def partner(rows):
        return jnp.where(step == 0, one_ref[rows, :], two_ref[rows, :])

    forward(lambda rows: a_ref[rows, :] * partner(rows), table_z, table_r, first_ref)
    middle(kernel_ref, table_r, first_ref, second_ref)

    def turned(i):
        quarter = lax.rem(i // 4 + shift, 4)
        return pl.ds(pl.multiple_of(quarter * 1024 + (i % 4) * 256, 256), 256)

    @pl.when(step == 0)
    def _():
        def emit(i, rows, value):
            out_ref[turned(i), :] = part_ref[rows, :] + one_ref[rows, :] * value

        backward(emit, table_z, table_r, second_ref)

    @pl.when(step == 1)
    def _():
        def emit(i, rows, value):
            out_ref[turned(i), :] += two_ref[rows, :] * value

        backward(emit, table_z, table_r, second_ref)


def plans():
    plan = np.zeros((2, 4, 6, 7), np.int32)
    for h in range(2):
        for j in range(4):
            if j < 3:
                first, second = ((0, 1), (0, 2), (1, 2))[j]
                own = [(first, 3 * h + second, 1, second, 1)]
                own += [(row, 3 * (1 - h) + j, 1, 0, 0) for row in range(3)]
            else:
                own = [(row, 3 * h + row, 1, 0, 0) for row in range(3)] + [(2, 3 * h + 2, 0, 0, 0)]
            for s, (row, b, valid, mirror, weight) in enumerate(own):
                plan[h, j, :, s] = (3 * h + row, b, valid, row, mirror, weight)
            for row in range(3):
                plan[h, j, :, 4 + row] = (3 * h + row, own[3][1], 1, row, 0, 0)
    return plan


def device(c, y, h):
    return c * N_PAIR + y * 2 + h


def routes():
    same_chip, near_side, far_side = [], [], []
    for c in range(N_BAND):
        beyond = (c + (1 if c % 2 else -1)) % N_BAND
        for y in range(4):
            for h in range(2):
                here = device(c, y, h)
                twin = (device(c ^ 1, y, h), here)
                same_chip.append(twin)
                near_side.append((device(beyond, y, h), here) if y < 3 else twin)
                far_side.append((device(beyond, y, 1 - h), here) if y < 3 else twin)
    return same_chip, near_side, far_side


def pair_route(dy, flip):
    return [(y * 2 + h, ((y + dy) % 4) * 2 + (h ^ flip)) for y in range(4) for h in range(2)]


def whole(rows=ROWS, columns=NZ):
    return pl.BlockSpec((rows, columns), lambda *_: (0, 0))


def body(orbitals):
    flat = orbitals.reshape(6, ROWS, NZ)
    pair = lax.axis_index("pair")
    y, h = pair // 2, pair % 2
    same_chip, near_side, far_side = routes()

    def fetched(choice, route):
        chosen = lax.dynamic_index_in_dim(flat, jnp.asarray(choice)[y], 0, keepdims=False)
        return lax.ppermute(chosen, ("band", "pair"), route)

    other = fetched((0, 1, 2, 3), same_chip)
    one = fetched((0, 2, 4, 4), near_side)
    two = fetched((1, 3, 5, 5), far_side)

    kernel = screened_kernel()
    table_z, table_r = tables()
    plan = jnp.asarray(plans())[h, y]
    scratch = [pltpu.VMEM((ROWS, NZ), f32)] * 2
    params = pltpu.CompilerParams(vmem_limit_bytes=VMEM_LIMIT)

    def cost(pairs):
        return pl.CostEstimate(flops=pairs * 5 * 10**9, bytes_accessed=pairs * 4 * 10**6, transcendentals=0)

    near = pl.pallas_call(
        near_kernel,
        out_shape=jax.ShapeDtypeStruct((3, ROWS, NZ), f32),
        grid_spec=pltpu.PrefetchScalarGridSpec(
            num_scalar_prefetch=1,
            grid=(7,),
            in_specs=[
                pl.BlockSpec((None, ROWS, NZ), lambda s, plan: (plan[0, s], 0, 0)),
                pl.BlockSpec((None, ROWS, NZ), lambda s, plan: (plan[1, s], 0, 0)),
                whole(),
                whole(),
                whole(256, 256),
                whole(256, 256),
            ],
            out_specs=pl.BlockSpec((3, ROWS, NZ), lambda *_: (0, 0, 0)),
            scratch_shapes=scratch,
        ),
        compiler_params=params,
        cost_estimate=cost(7),
    )(plan, flat, flat, other, kernel, table_z, table_r)

    def finished(row):
        where = jnp.stack([3 * h + row, 4 - y])
        return pl.pallas_call(
            far_kernel,
            out_shape=jax.ShapeDtypeStruct((ROWS, NZ), f32),
            grid_spec=pltpu.PrefetchScalarGridSpec(
                num_scalar_prefetch=1,
                grid=(2,),
                in_specs=[
                    pl.BlockSpec((None, ROWS, NZ), lambda s, where: (where[0], 0, 0)),
                    whole(),
                    whole(),
                    whole(),
                    whole(256, 256),
                    whole(256, 256),
                    pl.BlockSpec((None, ROWS, NZ), lambda *_: (row, 0, 0)),
                ],
                out_specs=whole(),
                scratch_shapes=scratch,
            ),
            compiler_params=params,
            cost_estimate=cost(2),
        )(where, flat, one, two, kernel, table_z, table_r, near)

    def summed(total):
        quarters = total.reshape(4, 2, 512, NZ)
        up, down = pair_route(1, 0), pair_route(-1, 0)
        from_below = lax.ppermute(quarters[2, 0], "pair", up)
        from_above = lax.ppermute(quarters[2, 1], "pair", down)
        above = jnp.stack([quarters[1, 0] + from_below, quarters[1, 1]])
        below = jnp.stack([quarters[3, 0], quarters[3, 1] + from_above])
        from_below = lax.ppermute(above, "pair", up)
        from_above = lax.ppermute(below, "pair", down)
        return quarters[0] + from_below + from_above

    mine, theirs = [], []
    for row in range(3):
        done = summed(finished(row))
        mine.append(lax.dynamic_index_in_dim(done, h, 0, keepdims=False))
        gone = lax.dynamic_index_in_dim(done, 1 - h, 0, keepdims=False)
        theirs.append(lax.ppermute(gone, "pair", pair_route(0, 1)))
    low = [jnp.where(h == 0, m, t) for m, t in zip(mine, theirs)]
    high = [jnp.where(h == 0, t, m) for m, t in zip(mine, theirs)]
    return jnp.stack(low + high).reshape(6, 8, NY, NZ)


def solution(mesh):
    return jax.shard_map(
        body,
        mesh=mesh,
        in_specs=(P("band", None, None, None),),
        out_specs=P("band", "pair", None, None),
        check_vma=False,
    )
```

```python
import math

import jax
import jax.numpy as jnp
import ml_dtypes
import numpy as np
from jax import lax
from jax.experimental import pallas as pl
from jax.experimental.pallas import tpu as pltpu
from jax.sharding import PartitionSpec as P

grid_spacing = 0.6
screening = 0.106

f32 = jnp.float32
bf16 = jnp.bfloat16
NX = 64
NY = 64
NZ = 128
ROWS = NX * NY
VMEM_LIMIT = 56 * 2**20
MESH = pl.DeviceIdType.MESH


def signed_freq(count):
    steps = np.arange(count)
    signed = np.where(steps <= count // 2, steps, steps - count)
    return signed * (2.0 * math.pi / (count * grid_spacing))


def screened_kernel():
    fx, fy, fz = signed_freq(NX), signed_freq(NY), signed_freq(NZ)
    square = fy[:, None, None] ** 2 + fx[None, :, None] ** 2 + fz[None, None, :] ** 2
    safe = np.where(square > 0, square, 1.0)
    value = 4.0 * math.pi / safe * -np.expm1(-safe / (4.0 * screening * screening))
    value = np.where(square > 0, value, math.pi / (screening * screening))
    value = (value * (-1.0 / (NX * NY * NZ))).astype(np.float32)
    return jnp.asarray(value.reshape(ROWS, NZ))


def cas(count):
    k = np.arange(count)
    angles = 2.0 * np.pi * ((k[:, None] * k[None, :]) % count) / count
    return np.cos(angles) + np.sin(angles)


def split_table(table):
    high = table.astype(ml_dtypes.bfloat16)
    low = (table - high.astype(np.float64)).astype(ml_dtypes.bfloat16)
    return high, low


def tables():
    high, low = split_table(cas(NZ))
    along_z = np.block([[high, low], [high, low]])
    high, low = split_table(cas(NY))
    zero = np.zeros_like(high)
    high = np.block([[high, zero], [zero, high]])
    low = np.block([[low, zero], [zero, low]])
    along_rows = np.block([[high, high], [low, low]])
    return jnp.asarray(along_z), jnp.asarray(along_rows)


def split(value):
    high = value.astype(bf16)
    low = (value - high.astype(f32)).astype(bf16)
    return high, low


def lanes_stage(value, table):
    high, low = split(value)
    out = jnp.dot(jnp.concatenate([high, low], axis=1), table, preferred_element_type=f32)
    return out[:, :NZ] + out[:, NZ:]


def rows_stage(tile, table):
    high, low = split(tile)
    out = jnp.dot(table, jnp.concatenate([high, low], axis=0), preferred_element_type=f32)
    return out[:128] + out[128:]


def to_tile(value):
    return jnp.concatenate([value[:128], value[128:]], axis=1)


def from_tile(tile):
    return jnp.concatenate([tile[:, :128], tile[:, 128:]], axis=0)


def forward(load, table_z, table_r, first_ref):
    def step(i, _):
        rows = pl.ds(pl.multiple_of(i * 256, 256), 256)
        value = lanes_stage(load(rows), table_z)
        first_ref[rows, :] = from_tile(rows_stage(to_tile(value), table_r))
        return 0

    lax.fori_loop(0, 16, step, 0, unroll=16)


def middle(kernel_ref, table_r, first_ref, second_ref):
    def step(i, _):
        c = [first_ref[pl.ds(i * 4 + q, 64, stride=64), :] for q in range(4)]
        left = jnp.concatenate([c[0], c[1]], axis=0)
        right = jnp.concatenate([c[2], c[3]], axis=0)
        tile = rows_stage(jnp.concatenate([left, right], axis=1), table_r)
        rows = pl.ds(pl.multiple_of(i * 256, 256), 256)
        tile = tile * to_tile(kernel_ref[rows, :])
        value = from_tile(rows_stage(tile, table_r))
        for q in range(4):
            second_ref[pl.ds(i * 4 + q, 64, stride=64), :] = value[q * 64 : (q + 1) * 64]
        return 0

    lax.fori_loop(0, 16, step, 0, unroll=16)


def backward(emit, table_z, table_r, second_ref):
    def step(i, _):
        rows = pl.ds(pl.multiple_of(i * 256, 256), 256)
        tile = rows_stage(to_tile(second_ref[rows, :]), table_r)
        emit(i, rows, lanes_stage(from_tile(tile), table_z))
        return 0

    lax.fori_loop(0, 16, step, 0, unroll=16)


def fused_kernel(
    orb_ref, kernel_in, z_ref, r_ref, out_ref,
    held, sums, first_ref, second_ref, kernel_ref,
    half_up, half_down, full_up, full_down, across,
    load_sem, in_send, in_recv, ring_send, ring_recv, flip_send, flip_recv, out_sem,
):
    band, pair = lax.axis_index("band"), lax.axis_index("pair")
    y, h = pair // 2, pair % 2
    last = y // 3
    odd = band % 2
    twin = band + 1 - 2 * odd
    beyond = (band + 15 + 2 * odd) % 16
    target = beyond + last * (twin - beyond)
    target_h = (1 - h) + last * (2 * h - 1)
    twin_id = (twin, pair)
    near_id = (target, pair)
    far_id = (target, y * 2 + target_h)
    up_id = (band, ((y + 1) % 4) * 2 + h)
    down_id = (band, ((y + 3) % 4) * 2 + h)
    flip_id = (band, y * 2 + 1 - h)

    def load(source, slot):
        return pltpu.make_async_copy(orb_ref.at[source], held.at[slot], load_sem.at[slot])

    loads = [load(3 * h + s, s) for s in range(3)] + [load(3 * (1 - h) + y - last, 3)]
    table_load = pltpu.make_async_copy(kernel_in, kernel_ref, load_sem.at[4])
    for copy in loads[:3]:
        copy.start()
    table_load.start()
    loads[3].start()

    barrier = pltpu.get_barrier_semaphore()
    for other in (twin_id, near_id, far_id, up_id, down_id, flip_id):
        pl.semaphore_signal(barrier, inc=1, device_id=other, device_id_type=MESH)
    pl.semaphore_wait(barrier, 6)

    def remote(source, target_ref, sends, receives, index, device):
        return pltpu.make_async_remote_copy(
            src_ref=source, dst_ref=target_ref, send_sem=sends.at[index], recv_sem=receives.at[index],
            device_id=device, device_id_type=MESH,
        )

    def half_in(source, slot, half, index, device):
        rows = pl.ds(half * 2048, 2048)
        return remote(orb_ref.at[source, rows, :], held.at[slot, rows, :], in_send, in_recv, index, device)

    from_twin = remote(orb_ref.at[y], held.at[4], in_send, in_recv, 0, twin_id)
    one = 2 * y - 2 * last
    first_in = [half_in(one, 5, 0, 1, near_id), half_in(one, 5, 1, 2, far_id)]
    second_in = [half_in(one + 1, 6, 0, 3, near_id), half_in(one + 1, 6, 1, 4, far_id)]
    from_twin.start()
    for copy in first_in:
        copy.start()

    sums[...] = jnp.zeros_like(sums)
    table_z, table_r = z_ref[...], r_ref[...]
    for copy in loads[:3]:
        copy.wait()
    table_load.wait()

    quarter = [pl.multiple_of(((y + q) % 4) * 1024, 1024) for q in range(4)]

    def ring(v, k):
        start, count, target_ref = (
            (quarter[2], 512, half_up),
            (quarter[2] + 512, 512, half_down),
            (quarter[1], 1024, full_up),
            (quarter[3], 1024, full_down),
        )[k]
        rows = pl.ds(pl.multiple_of(start, 512), count)
        device = (up_id, down_id)[k % 2]
        return remote(sums.at[v, rows, :], target_ref.at[v], ring_send, ring_recv, 4 * v + k, device)

    def flip(v):
        rows = pl.ds(pl.multiple_of(quarter[0] + (1 - h) * 512, 512), 512)
        return remote(sums.at[v, rows, :], across.at[v], flip_send, flip_recv, v, flip_id)

    def mine(v):
        rows = pl.ds(pl.multiple_of(quarter[0] + h * 512, 512), 512)
        return pltpu.make_async_copy(sums.at[v, rows, :], out_ref.at[3 * h + v], out_sem.at[v])

    def theirs(v):
        return pltpu.make_async_copy(across.at[v], out_ref.at[3 * (1 - h) + v], out_sem.at[3 + v])

    def ring_start(v):
        ring(v, 0).start()
        ring(v, 1).start()

    def ring_pass(v):
        ring(v, 0).wait_recv()
        rows = pl.ds(quarter[1], 512)
        sums[v, rows, :] += half_up[v]
        ring(v, 2).start()
        ring(v, 1).wait_recv()
        rows = pl.ds(quarter[3] + 512, 512)
        sums[v, rows, :] += half_down[v]
        ring(v, 3).start()

    def ring_end(v):
        ring(v, 2).wait_recv()
        ring(v, 3).wait_recv()
        rows = pl.ds(pl.multiple_of(quarter[0] + (1 - h) * 512, 512), 512)
        part = pl.ds(pl.multiple_of((1 - h) * 512, 512), 512)
        sums[v, rows, :] += full_up[v, part, :] + full_down[v, part, :]
        flip(v).start()
        rows = pl.ds(pl.multiple_of(quarter[0] + h * 512, 512), 512)
        part = pl.ds(pl.multiple_of(h * 512, 512), 512)
        sums[v, rows, :] += full_up[v, part, :] + full_down[v, part, :]
        mine(v).start()

    def solve(a, b, emit):
        forward(lambda rows: held[a, rows, :] * held[b, rows, :], table_z, table_r, first_ref)
        middle(kernel_ref, table_r, first_ref, second_ref)
        backward(emit, table_z, table_r, second_ref)

    @pl.when(y < 3)
    def _():
        a = y // 2
        b = (1 + (y + 1) // 2) * (1 - last)

        def emit(i, rows, value):
            sums[a, rows, :] += held[b, rows, :] * value
            sums[b, rows, :] += held[a, rows, :] * value

        solve(a, b, emit)

    loads[3].wait()

    def edge(e, _):
        late = e // 6
        a = (1 - late) * (e % 3) + late * ((e // 2) % 3)
        twin_part = (e // 3) % 2
        b = (1 - late) * ((1 - twin_part) * (last * a + (1 - last) * 3) + twin_part * 4) + late * (5 + e % 2)

        @pl.when(e == 3)
        def _():
            from_twin.wait_recv()
            for copy in second_in:
                copy.start()

        @pl.when(e == 6)
        def _():
            for copy in first_in:
                copy.wait_recv()

        @pl.when(e == 7)
        def _():
            for copy in second_in:
                copy.wait_recv()

        def emit(i, rows, value):
            sums[a, rows, :] += held[b, rows, :] * value

        solve(a, b, emit)

        @pl.when(e == 7)
        def _():
            ring_start(0)

        @pl.when(e == 8)
        def _():
            ring_pass(0)

        @pl.when(e == 9)
        def _():
            ring_start(1)

        @pl.when(e == 10)
        def _():
            ring_end(0)
            ring_pass(1)

        return 0

    lax.fori_loop(0, 12, edge, 0)
    ring_start(2)
    ring_end(1)
    ring_pass(2)
    ring_end(2)
    for v in range(3):
        flip(v).wait_recv()
        theirs(v).start()
    from_twin.wait_send()
    for copy in first_in + second_in:
        copy.wait_send()
    for v in range(3):
        for k in range(4):
            ring(v, k).wait_send()
        flip(v).wait_send()
        mine(v).wait()
        theirs(v).wait()


def body(orbitals):
    flat = orbitals.reshape(6, ROWS, NZ)
    table_z, table_r = tables()
    anywhere = pl.BlockSpec(memory_space=pl.ANY)
    resident = pl.BlockSpec(memory_space=pltpu.VMEM)

    def buffer(*shape):
        return pltpu.VMEM(shape, f32)

    out = pl.pallas_call(
        fused_kernel,
        out_shape=jax.ShapeDtypeStruct((6, 512, NZ), f32),
        in_specs=[anywhere, anywhere, resident, resident],
        out_specs=anywhere,
        scratch_shapes=[
            buffer(7, ROWS, NZ),
            buffer(3, ROWS, NZ),
            buffer(ROWS, NZ),
            buffer(ROWS, NZ),
            buffer(ROWS, NZ),
            buffer(3, 512, NZ),
            buffer(3, 512, NZ),
            buffer(3, 1024, NZ),
            buffer(3, 1024, NZ),
            buffer(3, 512, NZ),
            pltpu.SemaphoreType.DMA((5,)),
            pltpu.SemaphoreType.DMA((5,)),
            pltpu.SemaphoreType.DMA((5,)),
            pltpu.SemaphoreType.DMA((12,)),
            pltpu.SemaphoreType.DMA((12,)),
            pltpu.SemaphoreType.DMA((3,)),
            pltpu.SemaphoreType.DMA((3,)),
            pltpu.SemaphoreType.DMA((6,)),
        ],
        compiler_params=pltpu.CompilerParams(
            vmem_limit_bytes=VMEM_LIMIT, collective_id=0, has_side_effects=True
        ),
        cost_estimate=pl.CostEstimate(flops=65 * 10**9, bytes_accessed=30 * 10**6, transcendentals=0),
    )(flat, screened_kernel(), table_z, table_r)
    return out.reshape(6, 8, NY, NZ)


def solution(mesh):
    return jax.shard_map(
        body,
        mesh=mesh,
        in_specs=(P("band", None, None, None),),
        out_specs=P("band", "pair", None, None),
        check_vma=False,
    )
```

```python
import math

import jax
import jax.numpy as jnp
import ml_dtypes
import numpy as np
from jax import lax
from jax.experimental import pallas as pl
from jax.experimental.pallas import tpu as pltpu
from jax.sharding import PartitionSpec as P

grid_spacing = 0.6
screening = 0.106

f32 = jnp.float32
bf16 = jnp.bfloat16
NX = 64
NY = 64
NZ = 128
ROWS = NX * NY
VMEM_LIMIT = 56 * 2**20
MESH = pl.DeviceIdType.MESH


def signed_freq(count):
    steps = np.arange(count)
    signed = np.where(steps <= count // 2, steps, steps - count)
    return signed * (2.0 * math.pi / (count * grid_spacing))


def screened_kernel():
    fx, fy, fz = signed_freq(NX), signed_freq(NY), signed_freq(NZ)
    square = fy[:, None, None] ** 2 + fx[None, :, None] ** 2 + fz[None, None, :] ** 2
    safe = np.where(square > 0, square, 1.0)
    value = 4.0 * math.pi / safe * -np.expm1(-safe / (4.0 * screening * screening))
    value = np.where(square > 0, value, math.pi / (screening * screening))
    value = (value * (-1.0 / (NX * NY * NZ))).astype(np.float32)
    return jnp.asarray(value.reshape(ROWS, NZ))


def cas(count):
    k = np.arange(count)
    angles = 2.0 * np.pi * ((k[:, None] * k[None, :]) % count) / count
    return np.cos(angles) + np.sin(angles)


def split_table(table):
    high = table.astype(ml_dtypes.bfloat16)
    low = (table - high.astype(np.float64)).astype(ml_dtypes.bfloat16)
    return high, low


def tables():
    high, low = split_table(cas(NZ))
    along_z = np.block([[high, low], [high, low]])
    high, low = split_table(cas(NY))
    zero = np.zeros_like(high)
    high = np.block([[high, zero], [zero, high]])
    low = np.block([[low, zero], [zero, low]])
    along_rows = np.block([[high, high], [low, low]])
    return jnp.asarray(along_z), jnp.asarray(along_rows)


def split(value):
    high = value.astype(bf16)
    low = (value - high.astype(f32)).astype(bf16)
    return high, low


def lanes_stage(value, table):
    high, low = split(value)
    out = jnp.dot(jnp.concatenate([high, low], axis=1), table, preferred_element_type=f32)
    return out[:, :NZ] + out[:, NZ:]


def rows_stage(tile, table):
    high, low = split(tile)
    out = jnp.dot(table, jnp.concatenate([high, low], axis=0), preferred_element_type=f32)
    return out[:128] + out[128:]


def to_tile(value):
    return jnp.concatenate([value[:128], value[128:]], axis=1)


def from_tile(tile):
    return jnp.concatenate([tile[:, :128], tile[:, 128:]], axis=0)


def forward(load, table_z, table_r, first_ref):
    def step(i, _):
        rows = pl.ds(pl.multiple_of(i * 256, 256), 256)
        value = lanes_stage(load(rows), table_z)
        value = from_tile(rows_stage(to_tile(value), table_r))
        for q in range(4):
            first_ref[pl.ds(i * 4 + q, 64, stride=64), :] = value[q * 64 : (q + 1) * 64]
        return 0

    lax.fori_loop(0, 16, step, 0, unroll=16)


def middle(kernel_ref, table_r, first_ref, second_ref):
    def step(i, _):
        rows = pl.ds(pl.multiple_of(i * 256, 256), 256)
        tile = rows_stage(to_tile(first_ref[rows, :]), table_r)
        tile = tile * to_tile(kernel_ref[rows, :])
        value = from_tile(rows_stage(tile, table_r))
        for q in range(4):
            second_ref[pl.ds(i * 4 + q, 64, stride=64), :] = value[q * 64 : (q + 1) * 64]
        return 0

    lax.fori_loop(0, 16, step, 0, unroll=16)


def backward(emit, table_z, table_r, second_ref):
    def step(i, _):
        rows = pl.ds(pl.multiple_of(i * 256, 256), 256)
        tile = rows_stage(to_tile(second_ref[rows, :]), table_r)
        emit(i, rows, lanes_stage(from_tile(tile), table_z))
        return 0

    lax.fori_loop(0, 16, step, 0, unroll=16)


def fused_kernel(
    orb_ref, kernel_in, z_ref, r_ref, out_ref,
    held, sums, first_ref, second_ref, kernel_ref,
    half_up, half_down, full_up, full_down, across,
    load_sem, in_send, in_recv, ring_send, ring_recv, flip_send, flip_recv, out_sem,
):
    band, pair = lax.axis_index("band"), lax.axis_index("pair")
    y, h = pair // 2, pair % 2
    last = y // 3
    odd = band % 2
    twin = band + 1 - 2 * odd
    beyond = (band + 15 + 2 * odd) % 16
    crossing = (y + odd) % 2
    target = twin + crossing * (beyond - twin)
    target_h = h + crossing * (1 - 2 * h)
    twin_id = (twin, pair)
    near_id = (beyond, pair)
    far_id = (beyond, y * 2 + 1 - h)
    near_two_id = (target, pair)
    far_two_id = (target, y * 2 + target_h)
    up_id = (band, ((y + 1) % 4) * 2 + h)
    down_id = (band, ((y + 3) % 4) * 2 + h)
    flip_id = (band, y * 2 + 1 - h)

    def load(source, slot):
        return pltpu.make_async_copy(orb_ref.at[source], held.at[slot], load_sem.at[slot])

    loads = [load(3 * h + s, s) for s in range(3)] + [load(3 * (1 - h) + y - last, 3)]
    table_load = pltpu.make_async_copy(kernel_in, kernel_ref, load_sem.at[4])
    for copy in loads[:3]:
        copy.start()
    table_load.start()
    loads[3].start()

    barrier = pltpu.get_barrier_semaphore()
    for other in (twin_id, near_id, far_id, up_id, down_id, flip_id):
        pl.semaphore_signal(barrier, inc=1, device_id=other, device_id_type=MESH)
    pl.semaphore_wait(barrier, 6)

    def remote(source, target_ref, sends, receives, index, device):
        return pltpu.make_async_remote_copy(
            src_ref=source, dst_ref=target_ref, send_sem=sends.at[index], recv_sem=receives.at[index],
            device_id=device, device_id_type=MESH,
        )

    def half_in(source, slot, half, index, device):
        rows = pl.ds(half * 2048, 2048)
        return remote(orb_ref.at[source, rows, :], held.at[slot, rows, :], in_send, in_recv, index, device)

    from_twin = remote(orb_ref.at[y], held.at[4], in_send, in_recv, 0, twin_id)
    first_in = [half_in(y, 5, 0, 1, near_id), half_in(y, 5, 1, 2, far_id)]
    second_in = [half_in(4 + y // 2, 6, 0, 3, near_two_id), half_in(4 + y // 2, 6, 1, 4, far_two_id)]
    from_twin.start()
    for copy in first_in:
        copy.start()

    sums[...] = jnp.zeros_like(sums)
    table_z, table_r = z_ref[...], r_ref[...]
    for copy in loads[:3]:
        copy.wait()
    table_load.wait()

    quarter = [pl.multiple_of(((y + q) % 4) * 1024, 1024) for q in range(4)]

    def ring(v, k):
        start, count, target_ref = (
            (quarter[2], 512, half_up),
            (quarter[2] + 512, 512, half_down),
            (quarter[1], 1024, full_up),
            (quarter[3], 1024, full_down),
        )[k]
        rows = pl.ds(pl.multiple_of(start, 512), count)
        device = (up_id, down_id)[k % 2]
        return remote(sums.at[v, rows, :], target_ref.at[v], ring_send, ring_recv, 4 * v + k, device)

    def flip(v):
        rows = pl.ds(pl.multiple_of(quarter[0] + (1 - h) * 512, 512), 512)
        return remote(sums.at[v, rows, :], across.at[v], flip_send, flip_recv, v, flip_id)

    def mine(v):
        rows = pl.ds(pl.multiple_of(quarter[0] + h * 512, 512), 512)
        return pltpu.make_async_copy(sums.at[v, rows, :], out_ref.at[3 * h + v], out_sem.at[v])

    def theirs(v):
        return pltpu.make_async_copy(across.at[v], out_ref.at[3 * (1 - h) + v], out_sem.at[3 + v])

    def ring_start(v):
        ring(v, 0).start()
        ring(v, 1).start()

    def ring_pass(v):
        ring(v, 0).wait_recv()
        rows = pl.ds(quarter[1], 512)
        sums[v, rows, :] += half_up[v]
        ring(v, 2).start()
        ring(v, 1).wait_recv()
        rows = pl.ds(quarter[3] + 512, 512)
        sums[v, rows, :] += half_down[v]
        ring(v, 3).start()

    def ring_end(v):
        ring(v, 2).wait_recv()
        ring(v, 3).wait_recv()
        rows = pl.ds(pl.multiple_of(quarter[0] + (1 - h) * 512, 512), 512)
        part = pl.ds(pl.multiple_of((1 - h) * 512, 512), 512)
        sums[v, rows, :] += full_up[v, part, :] + full_down[v, part, :]
        flip(v).start()
        rows = pl.ds(pl.multiple_of(quarter[0] + h * 512, 512), 512)
        part = pl.ds(pl.multiple_of(h * 512, 512), 512)
        sums[v, rows, :] += full_up[v, part, :] + full_down[v, part, :]
        mine(v).start()

    def solve(a, b, emit):
        forward(lambda rows: held[a, rows, :] * held[b, rows, :], table_z, table_r, first_ref)
        middle(kernel_ref, table_r, first_ref, second_ref)
        backward(emit, table_z, table_r, second_ref)

    @pl.when(y < 3)
    def _():
        a = y // 2
        b = (1 + (y + 1) // 2) * (1 - last)

        def emit(i, rows, value):
            sums[a, rows, :] += held[b, rows, :] * value
            sums[b, rows, :] += held[a, rows, :] * value

        solve(a, b, emit)

    loads[3].wait()

    def edge(e, _):
        late, odd_step = e // 6, e % 2
        a = late * ((e + 3) // 3 - 2) + (1 - late) * (1 - odd_step) * (e // 2)
        own = last * a + (1 - last) * 3
        b = late * (4 + e % 3) + (1 - late) * (odd_step * (4 + e // 2) + (1 - odd_step) * own)

        @pl.when(e == 1)
        def _():
            from_twin.wait_recv()

        @pl.when(e == 2)
        def _():
            for copy in second_in:
                copy.start()

        @pl.when(e == 3)
        def _():
            for copy in first_in:
                copy.wait_recv()

        @pl.when(e == 5)
        def _():
            for copy in second_in:
                copy.wait_recv()

        def emit(i, rows, value):
            sums[a, rows, :] += held[b, rows, :] * value

        solve(a, b, emit)

        @pl.when(e == 5)
        def _():
            ring_start(0)

        @pl.when(e == 6)
        def _():
            ring_pass(0)

        @pl.when(e == 8)
        def _():
            ring_start(1)
            ring_end(0)

        @pl.when(e == 9)
        def _():
            ring_pass(1)

        return 0

    lax.fori_loop(0, 12, edge, 0)
    ring_start(2)
    ring_end(1)
    ring_pass(2)
    ring_end(2)
    for v in range(3):
        flip(v).wait_recv()
        theirs(v).start()
    from_twin.wait_send()
    for copy in first_in + second_in:
        copy.wait_send()
    for v in range(3):
        for k in range(4):
            ring(v, k).wait_send()
        flip(v).wait_send()
        mine(v).wait()
        theirs(v).wait()


def body(orbitals):
    flat = orbitals.reshape(6, ROWS, NZ)
    table_z, table_r = tables()
    anywhere = pl.BlockSpec(memory_space=pl.ANY)
    resident = pl.BlockSpec(memory_space=pltpu.VMEM)

    def buffer(*shape):
        return pltpu.VMEM(shape, f32)

    out = pl.pallas_call(
        fused_kernel,
        out_shape=jax.ShapeDtypeStruct((6, 512, NZ), f32),
        in_specs=[anywhere, anywhere, resident, resident],
        out_specs=anywhere,
        scratch_shapes=[
            buffer(7, ROWS, NZ),
            buffer(3, ROWS, NZ),
            buffer(ROWS, NZ),
            buffer(ROWS, NZ),
            buffer(ROWS, NZ),
            buffer(3, 512, NZ),
            buffer(3, 512, NZ),
            buffer(3, 1024, NZ),
            buffer(3, 1024, NZ),
            buffer(3, 512, NZ),
            pltpu.SemaphoreType.DMA((5,)),
            pltpu.SemaphoreType.DMA((5,)),
            pltpu.SemaphoreType.DMA((5,)),
            pltpu.SemaphoreType.DMA((12,)),
            pltpu.SemaphoreType.DMA((12,)),
            pltpu.SemaphoreType.DMA((3,)),
            pltpu.SemaphoreType.DMA((3,)),
            pltpu.SemaphoreType.DMA((6,)),
        ],
        compiler_params=pltpu.CompilerParams(
            vmem_limit_bytes=VMEM_LIMIT, collective_id=0, has_side_effects=True
        ),
        cost_estimate=pl.CostEstimate(flops=65 * 10**9, bytes_accessed=30 * 10**6, transcendentals=0),
    )(flat, screened_kernel(), table_z, table_r)
    return out.reshape(6, 8, NY, NZ)


def solution(mesh):
    return jax.shard_map(
        body,
        mesh=mesh,
        in_specs=(P("band", None, None, None),),
        out_specs=P("band", "pair", None, None),
        check_vma=False,
    )
```

```python
import math

import jax
import jax.numpy as jnp
import ml_dtypes
import numpy as np
from jax import lax
from jax.experimental import pallas as pl
from jax.experimental.pallas import tpu as pltpu
from jax.sharding import PartitionSpec as P

grid_spacing = 0.6
screening = 0.106

f32 = jnp.float32
bf16 = jnp.bfloat16
NX = 64
NY = 64
NZ = 128
ROWS = NX * NY
VMEM_LIMIT = 56 * 2**20
MESH = pl.DeviceIdType.MESH


def signed_freq(count):
    steps = np.arange(count)
    signed = np.where(steps <= count // 2, steps, steps - count)
    return signed * (2.0 * math.pi / (count * grid_spacing))


def screened_kernel():
    fx, fy, fz = signed_freq(NX), signed_freq(NY), signed_freq(NZ)
    square = fy[:, None, None] ** 2 + fx[None, :, None] ** 2 + fz[None, None, :] ** 2
    safe = np.where(square > 0, square, 1.0)
    value = 4.0 * math.pi / safe * -np.expm1(-safe / (4.0 * screening * screening))
    value = np.where(square > 0, value, math.pi / (screening * screening))
    value = (value * (-1.0 / (NX * NY * NZ))).astype(np.float32)
    return jnp.asarray(value.reshape(ROWS, NZ))


def cas(count):
    k = np.arange(count)
    angles = 2.0 * np.pi * ((k[:, None] * k[None, :]) % count) / count
    return np.cos(angles) + np.sin(angles)


def split_table(table):
    high = table.astype(ml_dtypes.bfloat16)
    low = (table - high.astype(np.float64)).astype(ml_dtypes.bfloat16)
    return high, low


def tables():
    high, low = split_table(cas(NZ))
    along_z = np.block([[high, low], [high, low]])
    high, low = split_table(cas(NY))
    zero = np.zeros_like(high)
    high = np.block([[high, zero], [zero, high]])
    low = np.block([[low, zero], [zero, low]])
    along_rows = np.block([[high, high], [low, low]])
    return jnp.asarray(along_z), jnp.asarray(along_rows)


def split(value):
    high = value.astype(bf16)
    low = (value - high.astype(f32)).astype(bf16)
    return high, low


def lanes_stage(value, table):
    high, low = split(value)
    out = jnp.dot(jnp.concatenate([high, low], axis=1), table, preferred_element_type=f32)
    return out[:, :NZ] + out[:, NZ:]


def rows_stage(tile, table):
    high, low = split(tile)
    out = jnp.dot(table, jnp.concatenate([high, low], axis=0), preferred_element_type=f32)
    return out[:128] + out[128:]


def to_tile(value):
    return jnp.concatenate([value[:128], value[128:]], axis=1)


def from_tile(tile):
    return jnp.concatenate([tile[:, :128], tile[:, 128:]], axis=0)


def forward(load, table_z, table_r, first_ref):
    def step(i, _):
        rows = pl.ds(pl.multiple_of(i * 256, 256), 256)
        value = lanes_stage(load(rows), table_z)
        value = from_tile(rows_stage(to_tile(value), table_r))
        for q in range(4):
            first_ref[pl.ds(i * 4 + q, 64, stride=64), :] = value[q * 64 : (q + 1) * 64]
        return 0

    lax.fori_loop(0, 16, step, 0, unroll=16)


def middle(kernel_ref, table_r, first_ref, second_ref):
    def step(i, _):
        rows = pl.ds(pl.multiple_of(i * 256, 256), 256)
        tile = rows_stage(to_tile(first_ref[rows, :]), table_r)
        tile = tile * to_tile(kernel_ref[rows, :])
        value = from_tile(rows_stage(tile, table_r))
        for q in range(4):
            second_ref[pl.ds(i * 4 + q, 64, stride=64), :] = value[q * 64 : (q + 1) * 64]
        return 0

    lax.fori_loop(0, 16, step, 0, unroll=16)


def backward(emit, table_z, table_r, second_ref):
    def step(i, _):
        rows = pl.ds(pl.multiple_of(i * 256, 256), 256)
        tile = rows_stage(to_tile(second_ref[rows, :]), table_r)
        emit(i, rows, lanes_stage(from_tile(tile), table_z))
        return 0

    lax.fori_loop(0, 16, step, 0, unroll=16)


def fused_kernel(
    orb_ref, kernel_in, z_ref, r_ref, out_ref,
    held, sums, first_ref, second_ref, kernel_ref,
    half_up, half_down, full_up, full_down, across,
    load_sem, in_send, in_recv, ring_send, ring_recv, flip_send, flip_recv, out_sem,
):
    band, pair = lax.axis_index("band"), lax.axis_index("pair")
    y, h = pair // 2, pair % 2
    last = y // 3
    odd = band % 2
    twin = band + 1 - 2 * odd
    beyond = (band + 15 + 2 * odd) % 16
    crossing = (y + odd) % 2
    target = twin + crossing * (beyond - twin)
    target_h = h + crossing * (1 - 2 * h)
    twin_id = (twin, pair)
    near_id = (beyond, pair)
    far_id = (beyond, y * 2 + 1 - h)
    near_two_id = (target, pair)
    far_two_id = (target, y * 2 + target_h)
    up_id = (band, ((y + 1) % 4) * 2 + h)
    down_id = (band, ((y + 3) % 4) * 2 + h)
    flip_id = (band, y * 2 + 1 - h)

    def load(source, slot):
        return pltpu.make_async_copy(orb_ref.at[source], held.at[slot], load_sem.at[slot])

    loads = [load(3 * h + s, s) for s in range(3)] + [load(3 * (1 - h) + y - last, 3)]
    table_load = pltpu.make_async_copy(kernel_in, kernel_ref, load_sem.at[4])
    for copy in loads[:3]:
        copy.start()
    table_load.start()
    loads[3].start()

    barrier = pltpu.get_barrier_semaphore()
    for other in (twin_id, near_id, far_id, up_id, down_id, flip_id):
        pl.semaphore_signal(barrier, inc=1, device_id=other, device_id_type=MESH)
    pl.semaphore_wait(barrier, 6)

    def remote(source, target_ref, sends, receives, index, device):
        return pltpu.make_async_remote_copy(
            src_ref=source, dst_ref=target_ref, send_sem=sends.at[index], recv_sem=receives.at[index],
            device_id=device, device_id_type=MESH,
        )

    def half_in(source, slot, half, index, device):
        rows = pl.ds(half * 2048, 2048)
        return remote(orb_ref.at[source, rows, :], held.at[slot, rows, :], in_send, in_recv, index, device)

    from_twin = remote(orb_ref.at[y], held.at[4], in_send, in_recv, 0, twin_id)
    first_in = [half_in(y, 5, 0, 1, near_id), half_in(y, 5, 1, 2, far_id)]
    second_in = [half_in(4 + y // 2, 6, 0, 3, near_two_id), half_in(4 + y // 2, 6, 1, 4, far_two_id)]
    from_twin.start()
    for copy in first_in:
        copy.start()

    sums[...] = jnp.zeros_like(sums)
    table_z, table_r = z_ref[...], r_ref[...]
    for copy in loads[:3]:
        copy.wait()
    table_load.wait()

    quarter = [pl.multiple_of(((y + q) % 4) * 1024, 1024) for q in range(4)]

    def ring(v, k):
        start, count, target_ref = (
            (quarter[2], 512, half_up),
            (quarter[2] + 512, 512, half_down),
            (quarter[1], 1024, full_up),
            (quarter[3], 1024, full_down),
        )[k]
        rows = pl.ds(pl.multiple_of(start, 512), count)
        device = (up_id, down_id)[k % 2]
        return remote(sums.at[v, rows, :], target_ref.at[v], ring_send, ring_recv, 4 * v + k, device)

    def flip(v):
        rows = pl.ds(pl.multiple_of(quarter[0] + (1 - h) * 512, 512), 512)
        return remote(sums.at[v, rows, :], across.at[v], flip_send, flip_recv, v, flip_id)

    def mine(v):
        rows = pl.ds(pl.multiple_of(quarter[0] + h * 512, 512), 512)
        return pltpu.make_async_copy(sums.at[v, rows, :], out_ref.at[3 * h + v], out_sem.at[v])

    def theirs(v):
        return pltpu.make_async_copy(across.at[v], out_ref.at[3 * (1 - h) + v], out_sem.at[3 + v])

    def ring_start(v):
        ring(v, 0).start()
        ring(v, 1).start()

    def ring_pass(v):
        ring(v, 0).wait_recv()
        rows = pl.ds(quarter[1], 512)
        sums[v, rows, :] += half_up[v]
        ring(v, 2).start()
        ring(v, 1).wait_recv()
        rows = pl.ds(quarter[3] + 512, 512)
        sums[v, rows, :] += half_down[v]
        ring(v, 3).start()

    def ring_end(v):
        ring(v, 2).wait_recv()
        ring(v, 3).wait_recv()
        rows = pl.ds(pl.multiple_of(quarter[0] + (1 - h) * 512, 512), 512)
        part = pl.ds(pl.multiple_of((1 - h) * 512, 512), 512)
        sums[v, rows, :] += full_up[v, part, :] + full_down[v, part, :]
        flip(v).start()
        rows = pl.ds(pl.multiple_of(quarter[0] + h * 512, 512), 512)
        part = pl.ds(pl.multiple_of(h * 512, 512), 512)
        sums[v, rows, :] += full_up[v, part, :] + full_down[v, part, :]
        mine(v).start()

    def solve(a, b, emit):
        def phase(k, _):
            @pl.when(k == 0)
            def _():
                forward(lambda rows: held[a, rows, :] * held[b, rows, :], table_z, table_r, first_ref)

            @pl.when(k == 1)
            def _():
                middle(kernel_ref, table_r, first_ref, second_ref)

            @pl.when(k == 2)
            def _():
                backward(emit, table_z, table_r, second_ref)

            return 0

        lax.fori_loop(0, 3, phase, 0)

    @pl.when(y < 3)
    def _():
        a = y // 2
        b = (1 + (y + 1) // 2) * (1 - last)

        def emit(i, rows, value):
            sums[a, rows, :] += held[b, rows, :] * value
            sums[b, rows, :] += held[a, rows, :] * value

        solve(a, b, emit)

    loads[3].wait()

    def edge(e, _):
        late, odd_step = e // 6, e % 2
        a = late * ((e + 3) // 3 - 2) + (1 - late) * (1 - odd_step) * (e // 2)
        own = last * a + (1 - last) * 3
        b = late * (4 + e % 3) + (1 - late) * (odd_step * (4 + e // 2) + (1 - odd_step) * own)

        @pl.when(e == 1)
        def _():
            from_twin.wait_recv()

        @pl.when(e == 2)
        def _():
            for copy in second_in:
                copy.start()

        @pl.when(e == 3)
        def _():
            for copy in first_in:
                copy.wait_recv()

        @pl.when(e == 5)
        def _():
            for copy in second_in:
                copy.wait_recv()

        def emit(i, rows, value):
            sums[a, rows, :] += held[b, rows, :] * value

        solve(a, b, emit)

        @pl.when(e == 5)
        def _():
            ring_start(0)

        @pl.when(e == 6)
        def _():
            ring_pass(0)

        @pl.when(e == 8)
        def _():
            ring_start(1)
            ring_end(0)

        @pl.when(e == 9)
        def _():
            ring_pass(1)

        return 0

    lax.fori_loop(0, 12, edge, 0)
    ring_start(2)
    ring_end(1)
    ring_pass(2)
    ring_end(2)
    for v in range(3):
        flip(v).wait_recv()
        theirs(v).start()
    from_twin.wait_send()
    for copy in first_in + second_in:
        copy.wait_send()
    for v in range(3):
        for k in range(4):
            ring(v, k).wait_send()
        flip(v).wait_send()
        mine(v).wait()
        theirs(v).wait()


def body(orbitals):
    flat = orbitals.reshape(6, ROWS, NZ)
    table_z, table_r = tables()
    anywhere = pl.BlockSpec(memory_space=pl.ANY)
    resident = pl.BlockSpec(memory_space=pltpu.VMEM)

    def buffer(*shape):
        return pltpu.VMEM(shape, f32)

    out = pl.pallas_call(
        fused_kernel,
        out_shape=jax.ShapeDtypeStruct((6, 512, NZ), f32),
        in_specs=[anywhere, anywhere, resident, resident],
        out_specs=anywhere,
        scratch_shapes=[
            buffer(7, ROWS, NZ),
            buffer(3, ROWS, NZ),
            buffer(ROWS, NZ),
            buffer(ROWS, NZ),
            buffer(ROWS, NZ),
            buffer(3, 512, NZ),
            buffer(3, 512, NZ),
            buffer(3, 1024, NZ),
            buffer(3, 1024, NZ),
            buffer(3, 512, NZ),
            pltpu.SemaphoreType.DMA((5,)),
            pltpu.SemaphoreType.DMA((5,)),
            pltpu.SemaphoreType.DMA((5,)),
            pltpu.SemaphoreType.DMA((12,)),
            pltpu.SemaphoreType.DMA((12,)),
            pltpu.SemaphoreType.DMA((3,)),
            pltpu.SemaphoreType.DMA((3,)),
            pltpu.SemaphoreType.DMA((6,)),
        ],
        compiler_params=pltpu.CompilerParams(
            vmem_limit_bytes=VMEM_LIMIT, collective_id=0, has_side_effects=True
        ),
        cost_estimate=pl.CostEstimate(flops=65 * 10**9, bytes_accessed=30 * 10**6, transcendentals=0),
    )(flat, screened_kernel(), table_z, table_r)
    return out.reshape(6, 8, NY, NZ)


def solution(mesh):
    return jax.shard_map(
        body,
        mesh=mesh,
        in_specs=(P("band", None, None, None),),
        out_specs=P("band", "pair", None, None),
        check_vma=False,
    )
```

```python
import math

import jax
import jax.numpy as jnp
import ml_dtypes
import numpy as np
from jax import lax
from jax.experimental import pallas as pl
from jax.experimental.pallas import tpu as pltpu
from jax.sharding import PartitionSpec as P

grid_spacing = 0.6
screening = 0.106

f32 = jnp.float32
bf16 = jnp.bfloat16
NX = 64
NY = 64
NZ = 128
ROWS = NX * NY
VMEM_LIMIT = 56 * 2**20
MESH = pl.DeviceIdType.MESH


def signed_freq(count):
    steps = np.arange(count)
    signed = np.where(steps <= count // 2, steps, steps - count)
    return signed * (2.0 * math.pi / (count * grid_spacing))


def screened_kernel():
    fx, fy, fz = signed_freq(NX), signed_freq(NY), signed_freq(NZ)
    square = fy[:, None, None] ** 2 + fx[None, :, None] ** 2 + fz[None, None, :] ** 2
    safe = np.where(square > 0, square, 1.0)
    value = 4.0 * math.pi / safe * -np.expm1(-safe / (4.0 * screening * screening))
    value = np.where(square > 0, value, math.pi / (screening * screening))
    value = (value * (-1.0 / (NX * NY * NZ))).astype(np.float32)
    return jnp.asarray(value.reshape(ROWS, NZ))


def cas(count):
    k = np.arange(count)
    angles = 2.0 * np.pi * ((k[:, None] * k[None, :]) % count) / count
    return np.cos(angles) + np.sin(angles)


def split_table(table):
    high = table.astype(ml_dtypes.bfloat16)
    low = (table - high.astype(np.float64)).astype(ml_dtypes.bfloat16)
    return high, low


def tables():
    high, low = split_table(cas(NZ))
    along_z = np.block([[high, low], [high, low]])
    high, low = split_table(cas(NY))
    zero = np.zeros_like(high)
    high = np.block([[high, zero], [zero, high]])
    low = np.block([[low, zero], [zero, low]])
    along_rows = np.block([[high, high], [low, low]])
    return jnp.asarray(along_z), jnp.asarray(along_rows)


def split(value):
    high = value.astype(bf16)
    low = (value - high.astype(f32)).astype(bf16)
    return high, low


def lanes_stage(value, table):
    high, low = split(value)
    out = jnp.dot(jnp.concatenate([high, low], axis=1), table, preferred_element_type=f32)
    return out[:, :NZ] + out[:, NZ:]


def rows_stage(tile, table):
    high, low = split(tile)
    out = jnp.dot(table, jnp.concatenate([high, low], axis=0), preferred_element_type=f32)
    return out[:128] + out[128:]


def to_tile(value):
    return jnp.concatenate([value[:128], value[128:]], axis=1)


def from_tile(tile):
    return jnp.concatenate([tile[:, :128], tile[:, 128:]], axis=0)


def store_turned(ref, group, value):
    turned = jnp.transpose(value.reshape(8, 8, 8, NZ), (1, 2, 0, 3))
    for high in range(8):
        for low in range(8):
            start = (high * 8 + low) * 64 + group * 8
            ref[pl.ds(pl.multiple_of(start, 8), 8), :] = turned[high, low]


def forward(load, table_z, table_r, first_ref):
    def step(i, _):
        rows = pl.ds(pl.multiple_of(i * 512, 512), 512)
        value = lanes_stage(load(rows), table_z)
        halves = [rows_stage(to_tile(value[:256]), table_r), rows_stage(to_tile(value[256:]), table_r)]
        store_turned(first_ref, i, jnp.concatenate([from_tile(tile) for tile in halves], axis=0))
        return 0

    lax.fori_loop(0, 8, step, 0, unroll=8)


def middle(kernel_ref, table_r, first_ref, second_ref):
    def step(i, _):
        halves = []
        for half in range(2):
            rows = pl.ds(pl.multiple_of(i * 512 + half * 256, 256), 256)
            tile = rows_stage(to_tile(first_ref[rows, :]), table_r)
            tile = tile * to_tile(kernel_ref[rows, :])
            halves.append(from_tile(rows_stage(tile, table_r)))
        store_turned(second_ref, i, jnp.concatenate(halves, axis=0))
        return 0

    lax.fori_loop(0, 8, step, 0, unroll=8)


def backward(emit, table_z, table_r, second_ref):
    def step(i, _):
        rows = pl.ds(pl.multiple_of(i * 256, 256), 256)
        tile = rows_stage(to_tile(second_ref[rows, :]), table_r)
        emit(i, rows, lanes_stage(from_tile(tile), table_z))
        return 0

    lax.fori_loop(0, 16, step, 0, unroll=16)


def fused_kernel(
    orb_ref, kernel_in, z_ref, r_ref, out_ref,
    held, sums, first_ref, second_ref, kernel_ref,
    half_up, half_down, full_up, full_down, across,
    load_sem, in_send, in_recv, ring_send, ring_recv, flip_send, flip_recv, out_sem,
):
    band, pair = lax.axis_index("band"), lax.axis_index("pair")
    y, h = pair // 2, pair % 2
    last = y // 3
    odd = band % 2
    twin = band + 1 - 2 * odd
    beyond = (band + 15 + 2 * odd) % 16
    crossing = (y + odd) % 2
    twin_id = (twin, pair)
    near_id = (beyond, pair)
    far_id = (beyond, y * 2 + 1 - h)
    aside_y = (y + 3) % 4
    aside_id = (beyond, aside_y * 2 + 1 - h)
    aside_from_id = (beyond, ((y + 1) % 4) * 2 + 1 - h)
    up_id = (band, ((y + 1) % 4) * 2 + h)
    down_id = (band, ((y + 3) % 4) * 2 + h)
    flip_id = (band, y * 2 + 1 - h)

    def load(source, slot):
        return pltpu.make_async_copy(orb_ref.at[source], held.at[slot], load_sem.at[slot])

    loads = [load(3 * h + s, s) for s in range(3)] + [load(3 * (1 - h) + y - last, 3)]
    table_load = pltpu.make_async_copy(kernel_in, kernel_ref, load_sem.at[4])
    for copy in loads[:3]:
        copy.start()
    table_load.start()
    loads[3].start()

    barrier = pltpu.get_barrier_semaphore()
    for other in (twin_id, near_id, far_id, aside_id, aside_from_id, up_id, down_id, flip_id):
        pl.semaphore_signal(barrier, inc=1, device_id=other, device_id_type=MESH)
    pl.semaphore_wait(barrier, 8)

    def remote(source, target_ref, sends, receives, index, device, arrival=None):
        return pltpu.make_async_remote_copy(
            src_ref=source, dst_ref=target_ref, send_sem=sends.at[index],
            recv_sem=receives.at[index if arrival is None else arrival],
            device_id=device, device_id_type=MESH,
        )

    def half_in(source, slot, half, index, device, arrival=None):
        rows = pl.ds(half * 2048, 2048)
        return remote(
            orb_ref.at[source, rows, :], held.at[slot, rows, :], in_send, in_recv, index, device, arrival
        )

    from_twin = remote(orb_ref.at[y], held.at[4], in_send, in_recv, 0, twin_id)
    first_in = [half_in(y, 5, 0, 1, near_id), half_in(y, 5, 1, 2, far_id)]
    second = 4 + y // 2
    crossing_in = half_in(second, 6, 0, 3, near_id)
    staying_in = [half_in(second, 6, 0, 3, twin_id), half_in(second, 6, 1, 4, twin_id)]
    aside_in = half_in(4 + aside_y // 2, 6, 1, 5, aside_id, 4)

    def second_start():
        @pl.when(crossing == 1)
        def _():
            crossing_in.start()

        @pl.when(crossing == 0)
        def _():
            aside_in.start()
            for copy in staying_in:
                copy.start()

    def second_sent():
        @pl.when(crossing == 1)
        def _():
            crossing_in.wait_send()

        @pl.when(crossing == 0)
        def _():
            aside_in.wait_send()
            for copy in staying_in:
                copy.wait_send()

    from_twin.start()
    for copy in first_in:
        copy.start()

    sums[...] = jnp.zeros_like(sums)
    table_z, table_r = z_ref[...], r_ref[...]
    for copy in loads[:3]:
        copy.wait()
    table_load.wait()

    quarter = [pl.multiple_of(((y + q) % 4) * 1024, 1024) for q in range(4)]

    def ring(v, k):
        start, count, target_ref = (
            (quarter[2], 512, half_up),
            (quarter[2] + 512, 512, half_down),
            (quarter[1], 1024, full_up),
            (quarter[3], 1024, full_down),
        )[k]
        rows = pl.ds(pl.multiple_of(start, 512), count)
        device = (up_id, down_id)[k % 2]
        return remote(sums.at[v, rows, :], target_ref.at[v], ring_send, ring_recv, 4 * v + k, device)

    def flip(v):
        rows = pl.ds(pl.multiple_of(quarter[0] + (1 - h) * 512, 512), 512)
        return remote(sums.at[v, rows, :], across.at[v], flip_send, flip_recv, v, flip_id)

    def mine(v):
        rows = pl.ds(pl.multiple_of(quarter[0] + h * 512, 512), 512)
        return pltpu.make_async_copy(sums.at[v, rows, :], out_ref.at[3 * h + v], out_sem.at[v])

    def theirs(v):
        return pltpu.make_async_copy(across.at[v], out_ref.at[3 * (1 - h) + v], out_sem.at[3 + v])

    def ring_start(v):
        ring(v, 0).start()
        ring(v, 1).start()

    def ring_pass(v):
        ring(v, 0).wait_recv()
        rows = pl.ds(quarter[1], 512)
        sums[v, rows, :] += half_up[v]
        ring(v, 2).start()
        ring(v, 1).wait_recv()
        rows = pl.ds(quarter[3] + 512, 512)
        sums[v, rows, :] += half_down[v]
        ring(v, 3).start()

    def ring_end(v):
        ring(v, 2).wait_recv()
        ring(v, 3).wait_recv()
        rows = pl.ds(pl.multiple_of(quarter[0] + (1 - h) * 512, 512), 512)
        part = pl.ds(pl.multiple_of((1 - h) * 512, 512), 512)
        sums[v, rows, :] += full_up[v, part, :] + full_down[v, part, :]
        flip(v).start()
        rows = pl.ds(pl.multiple_of(quarter[0] + h * 512, 512), 512)
        part = pl.ds(pl.multiple_of(h * 512, 512), 512)
        sums[v, rows, :] += full_up[v, part, :] + full_down[v, part, :]
        mine(v).start()

    def solve(a, b, emit):
        forward(lambda rows: held[a, rows, :] * held[b, rows, :], table_z, table_r, first_ref)
        middle(kernel_ref, table_r, first_ref, second_ref)
        backward(emit, table_z, table_r, second_ref)

    @pl.when(y < 3)
    def _():
        a = y // 2
        b = (1 + (y + 1) // 2) * (1 - last)

        def emit(i, rows, value):
            sums[a, rows, :] += held[b, rows, :] * value
            sums[b, rows, :] += held[a, rows, :] * value

        solve(a, b, emit)

    loads[3].wait()

    def edge(e, _):
        late, odd_step = e // 6, e % 2
        a = late * ((e + 3) // 3 - 2) + (1 - late) * (1 - odd_step) * (e // 2)
        own = last * a + (1 - last) * 3
        b = late * (4 + e % 3) + (1 - late) * (odd_step * (4 + e // 2) + (1 - odd_step) * own)

        @pl.when(e == 1)
        def _():
            from_twin.wait_recv()

        @pl.when(e == 2)
        def _():
            second_start()

        @pl.when(e == 3)
        def _():
            for copy in first_in:
                copy.wait_recv()

        @pl.when(e == 5)
        def _():
            for copy in staying_in:
                copy.wait_recv()

        def emit(i, rows, value):
            sums[a, rows, :] += held[b, rows, :] * value

        solve(a, b, emit)

        @pl.when(e == 5)
        def _():
            ring_start(0)

        @pl.when(e == 6)
        def _():
            ring_pass(0)

        @pl.when(e == 8)
        def _():
            ring_start(1)
            ring_end(0)

        @pl.when(e == 9)
        def _():
            ring_pass(1)

        return 0

    lax.fori_loop(0, 12, edge, 0)
    ring_start(2)
    ring_end(1)
    ring_pass(2)
    ring_end(2)
    for v in range(3):
        flip(v).wait_recv()
        theirs(v).start()
    from_twin.wait_send()
    for copy in first_in:
        copy.wait_send()
    second_sent()
    for v in range(3):
        for k in range(4):
            ring(v, k).wait_send()
        flip(v).wait_send()
        mine(v).wait()
        theirs(v).wait()


def body(orbitals):
    flat = orbitals.reshape(6, ROWS, NZ)
    table_z, table_r = tables()
    anywhere = pl.BlockSpec(memory_space=pl.ANY)
    resident = pl.BlockSpec(memory_space=pltpu.VMEM)

    def buffer(*shape):
        return pltpu.VMEM(shape, f32)

    out = pl.pallas_call(
        fused_kernel,
        out_shape=jax.ShapeDtypeStruct((6, 512, NZ), f32),
        in_specs=[anywhere, anywhere, resident, resident],
        out_specs=anywhere,
        scratch_shapes=[
            buffer(7, ROWS, NZ),
            buffer(3, ROWS, NZ),
            buffer(ROWS, NZ),
            buffer(ROWS, NZ),
            buffer(ROWS, NZ),
            buffer(3, 512, NZ),
            buffer(3, 512, NZ),
            buffer(3, 1024, NZ),
            buffer(3, 1024, NZ),
            buffer(3, 512, NZ),
            pltpu.SemaphoreType.DMA((5,)),
            pltpu.SemaphoreType.DMA((6,)),
            pltpu.SemaphoreType.DMA((5,)),
            pltpu.SemaphoreType.DMA((12,)),
            pltpu.SemaphoreType.DMA((12,)),
            pltpu.SemaphoreType.DMA((3,)),
            pltpu.SemaphoreType.DMA((3,)),
            pltpu.SemaphoreType.DMA((6,)),
        ],
        compiler_params=pltpu.CompilerParams(
            vmem_limit_bytes=VMEM_LIMIT, collective_id=0, has_side_effects=True
        ),
        cost_estimate=pl.CostEstimate(flops=65 * 10**9, bytes_accessed=30 * 10**6, transcendentals=0),
    )(flat, screened_kernel(), table_z, table_r)
    return out.reshape(6, 8, NY, NZ)


def solution(mesh):
    return jax.shard_map(
        body,
        mesh=mesh,
        in_specs=(P("band", None, None, None),),
        out_specs=P("band", "pair", None, None),
        check_vma=False,
    )
```

```python
import math

import jax
import jax.numpy as jnp
import ml_dtypes
import numpy as np
from jax import lax
from jax.experimental import pallas as pl
from jax.experimental.pallas import tpu as pltpu
from jax.sharding import PartitionSpec as P

grid_spacing = 0.6
screening = 0.106

f32 = jnp.float32
bf16 = jnp.bfloat16
NX = 64
NY = 64
NZ = 128
ROWS = NX * NY
VMEM_LIMIT = 56 * 2**20
MESH = pl.DeviceIdType.MESH


def signed_freq(count):
    steps = np.arange(count)
    signed = np.where(steps <= count // 2, steps, steps - count)
    return signed * (2.0 * math.pi / (count * grid_spacing))


def screened_kernel():
    fx, fy, fz = signed_freq(NX), signed_freq(NY), signed_freq(NZ)
    square = fy[:, None, None] ** 2 + fx[None, :, None] ** 2 + fz[None, None, :] ** 2
    safe = np.where(square > 0, square, 1.0)
    value = 4.0 * math.pi / safe * -np.expm1(-safe / (4.0 * screening * screening))
    value = np.where(square > 0, value, math.pi / (screening * screening))
    value = (value * (-1.0 / (NX * NY * NZ))).astype(np.float32)
    return jnp.asarray(value.reshape(ROWS, NZ))


def cas(count):
    k = np.arange(count)
    angles = 2.0 * np.pi * ((k[:, None] * k[None, :]) % count) / count
    return np.cos(angles) + np.sin(angles)


def split_table(table):
    high = table.astype(ml_dtypes.bfloat16)
    low = (table - high.astype(np.float64)).astype(ml_dtypes.bfloat16)
    return high, low


def tables():
    high, low = split_table(cas(NZ))
    along_z = np.block([[high, low], [high, low]])
    high, low = split_table(cas(NY))
    zero = np.zeros_like(high)
    high = np.block([[high, zero], [zero, high]])
    low = np.block([[low, zero], [zero, low]])
    along_rows = np.block([[high, high], [low, low]])
    return jnp.asarray(along_z), jnp.asarray(along_rows)


def split(value):
    high = value.astype(bf16)
    low = (value - high.astype(f32)).astype(bf16)
    return high, low


def lanes_stage(value, table):
    high, low = split(value)
    out = jnp.dot(jnp.concatenate([high, low], axis=1), table, preferred_element_type=f32)
    return out[:, :NZ] + out[:, NZ:]


def rows_stage(tile, table):
    high, low = split(tile)
    out = jnp.dot(table, jnp.concatenate([high, low], axis=0), preferred_element_type=f32)
    return out[:128] + out[128:]


def to_tile(value):
    return jnp.concatenate([value[:128], value[128:]], axis=1)


def from_tile(tile):
    return jnp.concatenate([tile[:, :128], tile[:, 128:]], axis=0)


def store_turned(ref, group, value):
    turned = jnp.transpose(value.reshape(8, 8, 8, NZ), (1, 2, 0, 3))
    for high in range(8):
        for low in range(8):
            start = (high * 8 + low) * 64 + group * 8
            ref[pl.ds(pl.multiple_of(start, 8), 8), :] = turned[high, low]


def forward(load, table_z, table_r, first_ref):
    def step(i, _):
        rows = pl.ds(pl.multiple_of(i * 512, 512), 512)
        value = lanes_stage(load(rows), table_z)
        halves = [rows_stage(to_tile(value[:256]), table_r), rows_stage(to_tile(value[256:]), table_r)]
        store_turned(first_ref, i, jnp.concatenate([from_tile(tile) for tile in halves], axis=0))
        return 0

    lax.fori_loop(0, 8, step, 0, unroll=8)


def middle(kernel_ref, table_r, first_ref, second_ref):
    def step(i, _):
        halves = []
        for half in range(2):
            rows = pl.ds(pl.multiple_of(i * 512 + half * 256, 256), 256)
            tile = rows_stage(to_tile(first_ref[rows, :]), table_r)
            tile = tile * to_tile(kernel_ref[rows, :])
            halves.append(from_tile(rows_stage(tile, table_r)))
        store_turned(second_ref, i, jnp.concatenate(halves, axis=0))
        return 0

    lax.fori_loop(0, 8, step, 0, unroll=8)


def backward(emit, table_z, table_r, second_ref):
    def step(i, _):
        rows = pl.ds(pl.multiple_of(i * 256, 256), 256)
        tile = rows_stage(to_tile(second_ref[rows, :]), table_r)
        emit(i, rows, lanes_stage(from_tile(tile), table_z))
        return 0

    lax.fori_loop(0, 16, step, 0, unroll=16)


def fused_kernel(
    orb_ref, kernel_in, z_ref, r_ref, out_ref,
    held, sums, first_ref, second_ref, kernel_ref, twin_part, side_part,
    load_sem, owned_send, owned_recv, in_send, in_recv, twin_send, twin_recv, side_send, side_recv,
    out_send, out_recv, out_sem,
):
    band, pair = lax.axis_index("band"), lax.axis_index("pair")
    y, h = pair // 2, pair % 2
    core = band % 2
    side, u = y // 2, y % 2
    home = core * side + (1 - core) * (1 - side)
    twin = band + 1 - 2 * core
    block = band - core + side
    keep = home * h + (1 - home) * (1 - h)
    near_y = y + 1 - 2 * u
    far_y = 3 - y
    twin_id = (twin, pair)
    side_id = (band, near_y * 2 + h)
    across_id = (band, far_y * 2 + h)
    flip_id = (twin, y * 2 + 1 - h)
    corner_id = (twin, far_y * 2 + 1 - h)

    matched = core * (1 - side) + (1 - core) * side
    to_y = matched * y + (1 - matched) * far_y
    to_h = matched * h + (1 - matched) * (1 - h)
    forward_way = 2 * core - 1
    to_home = ((band + 16 + forward_way) % 16, to_y * 2 + to_h)
    to_guest = ((band + 16 + 2 * forward_way) % 16, to_y * 2 + to_h)
    foreign = (band - core + 15 + 3 * side) % 16
    from_same = (foreign, pair)
    from_other = (foreign, far_y * 2 + 1 - h)

    def load(source, slot):
        return pltpu.make_async_copy(orb_ref.at[source], held.at[slot], load_sem.at[slot])

    owned_loads = [load(3 * h + v, v) for v in range(3)]
    loads = [
        load(home * (3 * (1 - h) + 2 * u) + (1 - home) * 3 * u, 3),
        load(home * (3 * (1 - h) + 1) + (1 - home) * (3 * u + 1), 4),
    ]
    guest_load = load(3 * u + 2, 5)
    table_load = pltpu.make_async_copy(kernel_in, kernel_ref, load_sem.at[6])

    @pl.when(home == 1)
    def _():
        for copy in owned_loads:
            copy.start()

    table_load.start()
    for copy in loads:
        copy.start()

    @pl.when(home == 0)
    def _():
        guest_load.start()

    barrier = pltpu.get_barrier_semaphore()
    partners = (twin_id, side_id, across_id, flip_id, corner_id, to_home, to_guest, from_same, from_other)
    for other in partners:
        pl.semaphore_signal(barrier, inc=1, device_id=other, device_id_type=MESH)
    pl.semaphore_wait(barrier, len(partners))

    def remote(source, target_ref, send_sem, recv_sem, device):
        return pltpu.make_async_remote_copy(
            src_ref=source, dst_ref=target_ref, send_sem=send_sem, recv_sem=recv_sem,
            device_id=device, device_id_type=MESH,
        )

    def owned_in(v):
        return remote(orb_ref.at[3 * h + v], held.at[v], owned_send.at[v], owned_recv.at[v], twin_id)

    def foreign_in(j):
        slot = (5, 6, 6)[j]
        rows = pl.ds(pl.multiple_of((1 - matched) * 2048, 2048), 2048)
        source = orb_ref.at[3 * (to_y % 2) + j, rows, :]
        arrival = in_recv.at[(slot - 5) * 2 + 1 - matched]
        return remote(source, held.at[slot, rows, :], in_send.at[j], arrival, to_guest if j == 2 else to_home)

    def foreign_wait(slot):
        for half in range(2):
            rows = pl.ds(half * 2048, 2048)
            ref = held.at[slot, rows, :]
            remote(ref, ref, in_send.at[0], in_recv.at[(slot - 5) * 2 + half], from_same).wait_recv()

    @pl.when(home == 1)
    def _():
        for v in range(3):
            owned_in(v).start()

    for j in (0, 2, 1):
        foreign_in(j).start()

    for v in range(3):
        sums[v] = jnp.zeros(sums.shape[1:], f32)
    table_z, table_r = z_ref[...], r_ref[...]

    @pl.when(home == 1)
    def _():
        for copy in owned_loads:
            copy.wait()

    @pl.when(home == 0)
    def _():
        owned_in(0).wait_recv()

    table_load.wait()

    def twin_copy(v):
        return remote(sums.at[v, :, 1 - keep], twin_part.at[v], twin_send.at[v], twin_recv.at[v], twin_id)

    def side_copy(v, k):
        row = (near_y, 3 - near_y)[k]
        index = 2 * v + k
        return remote(sums.at[v, row, keep], side_part.at[v, k], side_send.at[index], side_recv.at[index], side_id)

    def out_copy(v, k):
        row = (y, far_y)[k]
        return remote(
            sums.at[v, row, keep], out_ref.at[3 * h + v], out_send.at[2 * v + k], out_recv.at[3 * h + v],
            (block, row * 2 + keep),
        )

    def out_local(v):
        return pltpu.make_async_copy(sums.at[v, y, keep], out_ref.at[3 * h + v], out_sem.at[v])

    def pass_on(v):
        twin_copy(v).wait_recv()
        for k, row in enumerate((near_y, 3 - near_y)):
            sums[v, row, keep] += twin_part[v, row]
            side_copy(v, k).start()

    def finish(v):
        for k, row in ((1, far_y), (0, y)):
            side_copy(v, k).wait_recv()
            sums[v, row, keep] += twin_part[v, row] + side_part[v, k]
            if k == 1:
                out_copy(v, 1).start()
            else:

                @pl.when(home == 1)
                def _():
                    out_local(v).start()

                @pl.when(home == 0)
                def _():
                    out_copy(v, 0).start()

    def place(i):
        return i // 4, (i // 2) % 2, pl.ds(pl.multiple_of((i % 2) * 256, 256), 256)

    def solve(a, b, emit):
        forward(lambda rows: held[a, rows, :] * held[b, rows, :], table_z, table_r, first_ref)
        middle(kernel_ref, table_r, first_ref, second_ref)
        backward(emit, table_z, table_r, second_ref)

    def both(a, _):
        b = 2 - u

        def emit(i, rows, value):
            q, half, part = place(i)
            sums[a, q, half, part, :] += held[b, rows, :] * value
            sums[b, q, half, part, :] += held[a, rows, :] * value

        solve(a, b, emit)
        return 0

    lax.fori_loop(0, home * (2 - u), both, 0)
    for copy in loads:
        copy.wait()

    def edge(e, _):
        late = e // 8
        a = late * 2 + (1 - late) * ((e // 2) % 2)
        slot = late * (3 + e % 4) + (1 - late) * (3 + 2 * (e // 4) + e % 2)
        itself = home * u * ((7 - slot) // 3 - (6 - slot) // 3)
        b = slot + itself * (a - slot)

        @pl.when(e == 4)
        def _():
            @pl.when(home == 1)
            def _():
                foreign_wait(5)

            @pl.when(home == 0)
            def _():
                guest_load.wait()

        @pl.when(e == 5)
        def _():
            foreign_wait(6)

        @pl.when((1 - home) * e == 2)
        def _():
            owned_in(1).wait_recv()

        @pl.when((1 - home) * e == 8)
        def _():
            owned_in(2).wait_recv()

        def emit(i, rows, value):
            q, half, part = place(i)
            sums[a, q, half, part, :] += held[b, rows, :] * value

        solve(a, b, emit)

        @pl.when(e == 5)
        def _():
            twin_copy(0).start()

        @pl.when(e == 6)
        def _():
            pass_on(0)

        @pl.when(e == 7)
        def _():
            twin_copy(1).start()

        @pl.when(e == 8)
        def _():
            pass_on(1)

        @pl.when(e == 9)
        def _():
            finish(0)

        @pl.when(e == 11)
        def _():
            twin_copy(2).start()

        return 0

    lax.fori_loop(0, 12, edge, 0)
    pass_on(2)
    finish(1)
    finish(2)

    for v in range(3):
        remote(sums.at[v, y, keep], out_ref.at[3 * (1 - h) + v], out_send.at[0], out_recv.at[3 * (1 - h) + v], flip_id).wait_recv()

    @pl.when(home == 0)
    def _():
        for v in range(3):
            remote(sums.at[v, y, keep], out_ref.at[3 * h + v], out_send.at[0], out_recv.at[3 * h + v], flip_id).wait_recv()
            out_copy(v, 0).wait_send()

    @pl.when(home == 1)
    def _():
        for v in range(3):
            owned_in(v).wait_send()
            out_local(v).wait()

    for v in range(3):
        foreign_in(v).wait_send()
        twin_copy(v).wait_send()
        side_copy(v, 0).wait_send()
        side_copy(v, 1).wait_send()
        out_copy(v, 1).wait_send()


def body(orbitals):
    flat = orbitals.reshape(6, ROWS, NZ)
    table_z, table_r = tables()
    anywhere = pl.BlockSpec(memory_space=pl.ANY)
    resident = pl.BlockSpec(memory_space=pltpu.VMEM)

    def buffer(*shape):
        return pltpu.VMEM(shape, f32)

    out = pl.pallas_call(
        fused_kernel,
        out_shape=jax.ShapeDtypeStruct((6, 512, NZ), f32),
        in_specs=[anywhere, anywhere, resident, resident],
        out_specs=anywhere,
        scratch_shapes=[
            buffer(7, ROWS, NZ),
            buffer(3, 4, 2, 512, NZ),
            buffer(ROWS, NZ),
            buffer(ROWS, NZ),
            buffer(ROWS, NZ),
            buffer(3, 4, 512, NZ),
            buffer(3, 2, 512, NZ),
        ]
        + [pltpu.SemaphoreType.DMA((count,)) for count in (7, 3, 3, 3, 4, 3, 3, 6, 6, 6, 6, 3)],
        compiler_params=pltpu.CompilerParams(
            vmem_limit_bytes=VMEM_LIMIT, collective_id=0, has_side_effects=True
        ),
        cost_estimate=pl.CostEstimate(flops=65 * 10**9, bytes_accessed=30 * 10**6, transcendentals=0),
    )(flat, screened_kernel(), table_z, table_r)
    return out.reshape(6, 8, NY, NZ)


def solution(mesh):
    return jax.shard_map(
        body,
        mesh=mesh,
        in_specs=(P("band", None, None, None),),
        out_specs=P("band", "pair", None, None),
        check_vma=False,
    )
```

```python
import math

import jax
import jax.numpy as jnp
import ml_dtypes
import numpy as np
from jax import lax
from jax.experimental import pallas as pl
from jax.experimental.pallas import tpu as pltpu
from jax.sharding import PartitionSpec as P

grid_spacing = 0.6
screening = 0.106

f32 = jnp.float32
bf16 = jnp.bfloat16
NX = 64
NY = 64
NZ = 128
ROWS = NX * NY
VMEM_LIMIT = 56 * 2**20
MESH = pl.DeviceIdType.MESH


def signed_freq(count):
    steps = np.arange(count)
    signed = np.where(steps <= count // 2, steps, steps - count)
    return signed * (2.0 * math.pi / (count * grid_spacing))


def screened_kernel():
    fx, fy, fz = signed_freq(NX), signed_freq(NY), signed_freq(NZ)
    square = fy[:, None, None] ** 2 + fx[None, :, None] ** 2 + fz[None, None, :] ** 2
    safe = np.where(square > 0, square, 1.0)
    value = 4.0 * math.pi / safe * -np.expm1(-safe / (4.0 * screening * screening))
    value = np.where(square > 0, value, math.pi / (screening * screening))
    value = (value * (-1.0 / (NX * NY * NZ))).astype(np.float32)
    return jnp.asarray(value.reshape(ROWS, NZ))


def cas(count):
    k = np.arange(count)
    angles = 2.0 * np.pi * ((k[:, None] * k[None, :]) % count) / count
    return np.cos(angles) + np.sin(angles)


def split_table(table):
    high = table.astype(ml_dtypes.bfloat16)
    low = (table - high.astype(np.float64)).astype(ml_dtypes.bfloat16)
    return high, low


def tables():
    high, low = split_table(cas(NZ))
    along_z = np.block([[high, low], [high, low]])
    high, low = split_table(cas(NY))
    zero = np.zeros_like(high)
    high = np.block([[high, zero], [zero, high]])
    low = np.block([[low, zero], [zero, low]])
    along_rows = np.block([[high, high], [low, low]])
    return jnp.asarray(along_z), jnp.asarray(along_rows)


def split(value):
    high = value.astype(bf16)
    low = (value - high.astype(f32)).astype(bf16)
    return high, low


def lanes_stage(value, table):
    high, low = split(value)
    out = jnp.dot(jnp.concatenate([high, low], axis=1), table, preferred_element_type=f32)
    return out[:, :NZ] + out[:, NZ:]


def rows_stage(tile, table):
    high, low = split(tile)
    out = jnp.dot(table, jnp.concatenate([high, low], axis=0), preferred_element_type=f32)
    return out[:128] + out[128:]


def to_tile(value):
    return jnp.concatenate([value[:128], value[128:]], axis=1)


def from_tile(tile):
    return jnp.concatenate([tile[:, :128], tile[:, 128:]], axis=0)


def store_turned(ref, group, value):
    turned = jnp.transpose(value.reshape(8, 8, 8, NZ), (1, 2, 0, 3))
    for high in range(8):
        for low in range(8):
            start = (high * 8 + low) * 64 + group * 8
            ref[pl.ds(pl.multiple_of(start, 8), 8), :] = turned[high, low]


def forward(load, table_z, table_r, first_ref):
    def step(i, _):
        rows = pl.ds(pl.multiple_of(i * 512, 512), 512)
        value = lanes_stage(load(rows), table_z)
        halves = [rows_stage(to_tile(value[:256]), table_r), rows_stage(to_tile(value[256:]), table_r)]
        store_turned(first_ref, i, jnp.concatenate([from_tile(tile) for tile in halves], axis=0))
        return 0

    lax.fori_loop(0, 8, step, 0, unroll=8)


def middle(kernel_ref, table_r, first_ref, second_ref):
    def step(i, _):
        halves = []
        for half in range(2):
            rows = pl.ds(pl.multiple_of(i * 512 + half * 256, 256), 256)
            tile = rows_stage(to_tile(first_ref[rows, :]), table_r)
            tile = tile * to_tile(kernel_ref[rows, :])
            halves.append(from_tile(rows_stage(tile, table_r)))
        store_turned(second_ref, i, jnp.concatenate(halves, axis=0))
        return 0

    lax.fori_loop(0, 8, step, 0, unroll=8)


def backward(emit, table_z, table_r, second_ref):
    def step(i, _):
        rows = pl.ds(pl.multiple_of(i * 256, 256), 256)
        tile = rows_stage(to_tile(second_ref[rows, :]), table_r)
        emit(i, rows, lanes_stage(from_tile(tile), table_z))
        return 0

    lax.fori_loop(0, 16, step, 0, unroll=16)


def fused_kernel(
    orb_ref, kernel_in, z_ref, r_ref, out_ref,
    held, sums, first_ref, second_ref, kernel_ref, twin_part, side_part,
    load_sem, owned_send, owned_recv, in_send, in_recv, twin_send, twin_recv, side_send, side_recv,
    out_send, out_recv, out_sem,
):
    band, pair = lax.axis_index("band"), lax.axis_index("pair")
    y, h = pair // 2, pair % 2
    core = band % 2
    side, u = y // 2, y % 2
    home = core * side + (1 - core) * (1 - side)
    twin = band + 1 - 2 * core
    block = band - core + side
    keep = home * h + (1 - home) * (1 - h)
    near_y = y + 1 - 2 * u
    far_y = 3 - y
    twin_id = (twin, pair)
    side_id = (band, near_y * 2 + h)
    across_id = (band, far_y * 2 + h)
    flip_id = (twin, y * 2 + 1 - h)
    corner_id = (twin, far_y * 2 + 1 - h)

    matched = core * (1 - side) + (1 - core) * side
    to_y = matched * y + (1 - matched) * far_y
    to_h = matched * h + (1 - matched) * (1 - h)
    forward_way = 2 * core - 1
    to_home = ((band + 16 + forward_way) % 16, to_y * 2 + to_h)
    to_guest = ((band + 16 + 2 * forward_way) % 16, to_y * 2 + to_h)
    foreign = (band - core + 15 + 3 * side) % 16
    from_same = (foreign, pair)
    from_other = (foreign, far_y * 2 + 1 - h)

    def load(source, slot):
        return pltpu.make_async_copy(orb_ref.at[source], held.at[slot], load_sem.at[slot])

    owned_loads = [load(3 * h + v, v) for v in range(3)]
    loads = [
        load(home * (3 * (1 - h) + 2 * u) + (1 - home) * 3 * u, 3),
        load(home * (3 * (1 - h) + 1) + (1 - home) * (3 * u + 1), 4),
    ]
    guest_load = load(3 * u + 2, 5)
    table_load = pltpu.make_async_copy(kernel_in, kernel_ref, load_sem.at[6])

    @pl.when(home == 1)
    def _():
        for copy in owned_loads:
            copy.start()

    table_load.start()
    for copy in loads:
        copy.start()

    @pl.when(home == 0)
    def _():
        guest_load.start()

    barrier = pltpu.get_barrier_semaphore()
    partners = (twin_id, side_id, across_id, flip_id, corner_id, to_home, to_guest, from_same, from_other)
    for other in partners:
        pl.semaphore_signal(barrier, inc=1, device_id=other, device_id_type=MESH)
    pl.semaphore_wait(barrier, len(partners))

    def remote(source, target_ref, send_sem, recv_sem, device):
        return pltpu.make_async_remote_copy(
            src_ref=source, dst_ref=target_ref, send_sem=send_sem, recv_sem=recv_sem,
            device_id=device, device_id_type=MESH,
        )

    def owned_in(v):
        return remote(orb_ref.at[3 * h + v], held.at[v], owned_send.at[v], owned_recv.at[v], twin_id)

    def foreign_in(j):
        slot = (5, 6, 6)[j]
        rows = pl.ds(pl.multiple_of((1 - matched) * 2048, 2048), 2048)
        source = orb_ref.at[3 * (to_y % 2) + j, rows, :]
        arrival = in_recv.at[(slot - 5) * 2 + 1 - matched]
        return remote(source, held.at[slot, rows, :], in_send.at[j], arrival, to_guest if j == 2 else to_home)

    def foreign_wait(slot):
        for half in range(2):
            rows = pl.ds(half * 2048, 2048)
            ref = held.at[slot, rows, :]
            remote(ref, ref, in_send.at[0], in_recv.at[(slot - 5) * 2 + half], from_same).wait_recv()

    @pl.when(home == 1)
    def _():
        for v in range(3):
            owned_in(v).start()

    for j in (0, 2):
        foreign_in(j).start()

    for v in range(3):
        sums[v] = jnp.zeros(sums.shape[1:], f32)
    table_z, table_r = z_ref[...], r_ref[...]

    @pl.when(home == 1)
    def _():
        for copy in owned_loads:
            copy.wait()

    @pl.when(home == 0)
    def _():
        owned_in(0).wait_recv()

    table_load.wait()

    def twin_copy(v):
        return remote(sums.at[v, :, 1 - keep], twin_part.at[v], twin_send.at[v], twin_recv.at[v], twin_id)

    def side_copy(v, k):
        row = (near_y, 3 - near_y)[k]
        index = 2 * v + k
        return remote(sums.at[v, row, keep], side_part.at[v, k], side_send.at[index], side_recv.at[index], side_id)

    def out_copy(v, k):
        row = (y, far_y)[k]
        return remote(
            sums.at[v, row, keep], out_ref.at[3 * h + v], out_send.at[2 * v + k], out_recv.at[3 * h + v],
            (block, row * 2 + keep),
        )

    def out_local(v):
        return pltpu.make_async_copy(sums.at[v, y, keep], out_ref.at[3 * h + v], out_sem.at[v])

    def pass_on(v):
        twin_copy(v).wait_recv()
        for k, row in ((1, 3 - near_y), (0, near_y)):
            sums[v, row, keep] += twin_part[v, row]
            side_copy(v, k).start()

    def finish(v):
        for k, row in ((1, far_y), (0, y)):
            side_copy(v, k).wait_recv()
            sums[v, row, keep] += twin_part[v, row] + side_part[v, k]
            if k == 1:
                out_copy(v, 1).start()
            else:

                @pl.when(home == 1)
                def _():
                    out_local(v).start()

                @pl.when(home == 0)
                def _():
                    out_copy(v, 0).start()

    def place(i):
        return i // 4, (i // 2) % 2, pl.ds(pl.multiple_of((i % 2) * 256, 256), 256)

    def solve(a, b, emit):
        forward(lambda rows: held[a, rows, :] * held[b, rows, :], table_z, table_r, first_ref)
        middle(kernel_ref, table_r, first_ref, second_ref)
        backward(emit, table_z, table_r, second_ref)

    def both(a, b):
        def emit(i, rows, value):
            q, half, part = place(i)
            sums[a, q, half, part, :] += held[b, rows, :] * value
            sums[b, q, half, part, :] += held[a, rows, :] * value

        solve(a, b, emit)

    for copy in loads:
        copy.wait()

    def edge(e, _):
        late, mid = e // 8, (e // 4) % 2
        a = late * 2 + (1 - late) * ((1 - mid) * ((e // 2) % 2) + mid * (e % 2))
        slot = 3 + late * (e % 4) + (1 - late) * ((1 - mid) * (e % 2) + mid * (2 + (e // 2) % 2))
        itself = home * u * ((7 - slot) // 3 - (6 - slot) // 3)
        b = slot + itself * (a - slot)

        @pl.when((1 - home) * e == 2)
        def _():
            owned_in(1).wait_recv()

        @pl.when(e == 3)
        def _():
            foreign_in(1).start()

        @pl.when(e == 4)
        def _():
            @pl.when(home == 1)
            def _():
                foreign_wait(5)

            @pl.when(home == 0)
            def _():
                guest_load.wait()
                owned_in(2).wait_recv()

        @pl.when(e + 100 * (1 - home) * u == 4 * (1 - home))
        def _():
            both(1 - home, home * (2 - u) + (1 - home) * 2)

        @pl.when(e == 6)
        def _():
            foreign_wait(6)

        def emit(i, rows, value):
            q, half, part = place(i)
            sums[a, q, half, part, :] += held[b, rows, :] * value

        solve(a, b, emit)

        @pl.when(e == 6)
        def _():
            twin_copy(0).start()

        @pl.when(e == 7)
        def _():
            twin_copy(1).start()
            pass_on(0)

        @pl.when(e == 8)
        def _():
            pass_on(1)

        @pl.when(e == 10)
        def _():
            finish(0)

        @pl.when(e == 11)
        def _():
            twin_copy(2).start()

        return 0

    lax.fori_loop(0, 12, edge, 0)
    pass_on(2)
    finish(1)
    finish(2)

    for v in range(3):
        remote(sums.at[v, y, keep], out_ref.at[3 * (1 - h) + v], out_send.at[0], out_recv.at[3 * (1 - h) + v], flip_id).wait_recv()

    @pl.when(home == 0)
    def _():
        for v in range(3):
            remote(sums.at[v, y, keep], out_ref.at[3 * h + v], out_send.at[0], out_recv.at[3 * h + v], flip_id).wait_recv()
            out_copy(v, 0).wait_send()

    @pl.when(home == 1)
    def _():
        for v in range(3):
            owned_in(v).wait_send()
            out_local(v).wait()

    for v in range(3):
        foreign_in(v).wait_send()
        twin_copy(v).wait_send()
        side_copy(v, 0).wait_send()
        side_copy(v, 1).wait_send()
        out_copy(v, 1).wait_send()


def body(orbitals):
    flat = orbitals.reshape(6, ROWS, NZ)
    table_z, table_r = tables()
    anywhere = pl.BlockSpec(memory_space=pl.ANY)
    resident = pl.BlockSpec(memory_space=pltpu.VMEM)

    def buffer(*shape):
        return pltpu.VMEM(shape, f32)

    out = pl.pallas_call(
        fused_kernel,
        out_shape=jax.ShapeDtypeStruct((6, 512, NZ), f32),
        in_specs=[anywhere, anywhere, resident, resident],
        out_specs=anywhere,
        scratch_shapes=[
            buffer(7, ROWS, NZ),
            buffer(3, 4, 2, 512, NZ),
            buffer(ROWS, NZ),
            buffer(ROWS, NZ),
            buffer(ROWS, NZ),
            buffer(3, 4, 512, NZ),
            buffer(3, 2, 512, NZ),
        ]
        + [pltpu.SemaphoreType.DMA((count,)) for count in (7, 3, 3, 3, 4, 3, 3, 6, 6, 6, 6, 3)],
        compiler_params=pltpu.CompilerParams(
            vmem_limit_bytes=VMEM_LIMIT, collective_id=0, has_side_effects=True
        ),
        cost_estimate=pl.CostEstimate(flops=65 * 10**9, bytes_accessed=30 * 10**6, transcendentals=0),
    )(flat, screened_kernel(), table_z, table_r)
    return out.reshape(6, 8, NY, NZ)


def solution(mesh):
    return jax.shard_map(
        body,
        mesh=mesh,
        in_specs=(P("band", None, None, None),),
        out_specs=P("band", "pair", None, None),
        check_vma=False,
    )
```

```python
import math

import jax
import jax.numpy as jnp
import ml_dtypes
import numpy as np
from jax import lax
from jax.experimental import pallas as pl
from jax.experimental.pallas import tpu as pltpu
from jax.sharding import PartitionSpec as P

grid_spacing = 0.6
screening = 0.106

f32 = jnp.float32
bf16 = jnp.bfloat16
NX = 64
NY = 64
NZ = 128
ROWS = NX * NY
VMEM_LIMIT = 56 * 2**20
MESH = pl.DeviceIdType.MESH


def signed_freq(count):
    steps = np.arange(count)
    signed = np.where(steps <= count // 2, steps, steps - count)
    return signed * (2.0 * math.pi / (count * grid_spacing))


def screened_kernel():
    fx, fy, fz = signed_freq(NX), signed_freq(NY), signed_freq(NZ)
    square = fy[:, None, None] ** 2 + fx[None, :, None] ** 2 + fz[None, None, :] ** 2
    safe = np.where(square > 0, square, 1.0)
    value = 4.0 * math.pi / safe * -np.expm1(-safe / (4.0 * screening * screening))
    value = np.where(square > 0, value, math.pi / (screening * screening))
    value = (value * (-1.0 / (NX * NY * NZ))).astype(np.float32)
    return jnp.asarray(value.reshape(ROWS, NZ))


def cas(count):
    k = np.arange(count)
    angles = 2.0 * np.pi * ((k[:, None] * k[None, :]) % count) / count
    return np.cos(angles) + np.sin(angles)


def split_table(table):
    high = table.astype(ml_dtypes.bfloat16)
    low = (table - high.astype(np.float64)).astype(ml_dtypes.bfloat16)
    return high, low


def tables():
    high, low = split_table(cas(NZ))
    along_z = np.block([[high, low], [high, low]])
    high, low = split_table(cas(NY))
    zero = np.zeros_like(high)
    high = np.block([[high, zero], [zero, high]])
    low = np.block([[low, zero], [zero, low]])
    along_rows = np.block([[high, high], [low, low]])
    return jnp.asarray(along_z), jnp.asarray(along_rows)


def split(value):
    high = value.astype(bf16)
    low = (value - high.astype(f32)).astype(bf16)
    return high, low


def lanes_stage(value, table):
    high, low = split(value)
    out = jnp.dot(jnp.concatenate([high, low], axis=1), table, preferred_element_type=f32)
    return out[:, :NZ] + out[:, NZ:]


def rows_stage(tile, table):
    high, low = split(tile)
    out = jnp.dot(table, jnp.concatenate([high, low], axis=0), preferred_element_type=f32)
    return out[:128] + out[128:]


def to_tile(value):
    return jnp.concatenate([value[:128], value[128:]], axis=1)


def from_tile(tile):
    return jnp.concatenate([tile[:, :128], tile[:, 128:]], axis=0)


def store_turned(ref, group, value):
    turned = jnp.transpose(value.reshape(8, 8, 8, NZ), (1, 2, 0, 3))
    for high in range(8):
        for low in range(8):
            start = (high * 8 + low) * 64 + group * 8
            ref[pl.ds(pl.multiple_of(start, 8), 8), :] = turned[high, low]


def forward(load, table_z, table_r, first_ref):
    def step(i, _):
        rows = pl.ds(pl.multiple_of(i * 512, 512), 512)
        value = lanes_stage(load(rows), table_z)
        halves = [rows_stage(to_tile(value[:256]), table_r), rows_stage(to_tile(value[256:]), table_r)]
        store_turned(first_ref, i, jnp.concatenate([from_tile(tile) for tile in halves], axis=0))
        return 0

    lax.fori_loop(0, 8, step, 0, unroll=8)


def middle(kernel_ref, table_r, first_ref, second_ref):
    def step(i, _):
        halves = []
        for half in range(2):
            rows = pl.ds(pl.multiple_of(i * 512 + half * 256, 256), 256)
            tile = rows_stage(to_tile(first_ref[rows, :]), table_r)
            tile = tile * to_tile(kernel_ref[rows, :])
            halves.append(from_tile(rows_stage(tile, table_r)))
        store_turned(second_ref, i, jnp.concatenate(halves, axis=0))
        return 0

    lax.fori_loop(0, 8, step, 0, unroll=8)


def backward(emit, table_z, table_r, second_ref):
    def step(i, _):
        rows = pl.ds(pl.multiple_of(i * 256, 256), 256)
        tile = rows_stage(to_tile(second_ref[rows, :]), table_r)
        emit(i, rows, lanes_stage(from_tile(tile), table_z))
        return 0

    lax.fori_loop(0, 16, step, 0, unroll=16)


def fused_kernel(
    orb_ref, kernel_in, z_ref, r_ref, out_ref,
    held, sums, first_ref, second_ref, kernel_ref, twin_part, side_part,
    load_sem, owned_send, owned_recv, in_send, in_recv, twin_send, twin_recv, side_send, side_recv,
    out_send, out_recv, out_sem,
):
    band, pair = lax.axis_index("band"), lax.axis_index("pair")
    y, h = pair // 2, pair % 2
    core = band % 2
    side, u = y // 2, y % 2
    home = core * side + (1 - core) * (1 - side)
    twin = band + 1 - 2 * core
    block = band - core + side
    keep = home * h + (1 - home) * (1 - h)
    near_y = y + 1 - 2 * u
    far_y = 3 - y
    twin_id = (twin, pair)
    side_id = (band, near_y * 2 + h)
    across_id = (band, far_y * 2 + h)
    flip_id = (twin, y * 2 + 1 - h)
    corner_id = (twin, far_y * 2 + 1 - h)

    matched = core * (1 - side) + (1 - core) * side
    to_y = matched * y + (1 - matched) * far_y
    to_h = matched * h + (1 - matched) * (1 - h)
    forward_way = 2 * core - 1
    to_home = ((band + 16 + forward_way) % 16, to_y * 2 + to_h)
    to_guest = ((band + 16 + 2 * forward_way) % 16, to_y * 2 + to_h)
    foreign = (band - core + 15 + 3 * side) % 16
    from_same = (foreign, pair)
    from_other = (foreign, far_y * 2 + 1 - h)

    def load(source, slot):
        return pltpu.make_async_copy(orb_ref.at[source], held.at[slot], load_sem.at[slot])

    owned_loads = [load(3 * h + v, v) for v in range(3)]
    loads = [
        load(home * (3 * (1 - h) + 2 * u) + (1 - home) * 3 * u, 3),
        load(home * (3 * (1 - h) + 1) + (1 - home) * (3 * u + 1), 4),
    ]
    guest_load = load(3 * u + 2, 5)
    table_load = pltpu.make_async_copy(kernel_in, kernel_ref, load_sem.at[6])

    @pl.when(home == 1)
    def _():
        for copy in owned_loads:
            copy.start()

    table_load.start()
    for copy in loads:
        copy.start()

    @pl.when(home == 0)
    def _():
        guest_load.start()

    barrier = pltpu.get_barrier_semaphore()
    partners = (twin_id, side_id, across_id, flip_id, corner_id, to_home, to_guest, from_same, from_other)
    for other in partners:
        pl.semaphore_signal(barrier, inc=1, device_id=other, device_id_type=MESH)
    pl.semaphore_wait(barrier, len(partners))

    def remote(source, target_ref, send_sem, recv_sem, device):
        return pltpu.make_async_remote_copy(
            src_ref=source, dst_ref=target_ref, send_sem=send_sem, recv_sem=recv_sem,
            device_id=device, device_id_type=MESH,
        )

    def owned_in(v):
        return remote(orb_ref.at[3 * h + v], held.at[v], owned_send.at[v], owned_recv.at[v], twin_id)

    def foreign_in(j):
        slot = (5, 6, 6)[j]
        rows = pl.ds(pl.multiple_of((1 - matched) * 2048, 2048), 2048)
        source = orb_ref.at[3 * (to_y % 2) + j, rows, :]
        arrival = in_recv.at[(slot - 5) * 2 + 1 - matched]
        return remote(source, held.at[slot, rows, :], in_send.at[j], arrival, to_guest if j == 2 else to_home)

    def foreign_wait(slot):
        for half in range(2):
            rows = pl.ds(half * 2048, 2048)
            ref = held.at[slot, rows, :]
            remote(ref, ref, in_send.at[0], in_recv.at[(slot - 5) * 2 + half], from_same).wait_recv()

    @pl.when(home == 1)
    def _():
        for v in range(3):
            owned_in(v).start()

    for j in (0, 2):
        foreign_in(j).start()

    for v in range(3):
        sums[v] = jnp.zeros(sums.shape[1:], f32)
    table_z, table_r = z_ref[...], r_ref[...]

    @pl.when(home == 1)
    def _():
        for copy in owned_loads:
            copy.wait()

    @pl.when(home == 0)
    def _():
        owned_in(0).wait_recv()

    table_load.wait()

    def twin_copy(v):
        return remote(sums.at[v, :, 1 - keep], twin_part.at[v], twin_send.at[v], twin_recv.at[v], twin_id)

    def side_copy(v, k):
        row = (near_y, 3 - near_y)[k]
        index = 2 * v + k
        return remote(sums.at[v, row, keep], side_part.at[v, k], side_send.at[index], side_recv.at[index], side_id)

    def out_copy(v, k):
        row = (y, far_y)[k]
        return remote(
            sums.at[v, row, keep], out_ref.at[3 * h + v], out_send.at[2 * v + k], out_recv.at[3 * h + v],
            (block, row * 2 + keep),
        )

    def out_local(v):
        return pltpu.make_async_copy(sums.at[v, y, keep], out_ref.at[3 * h + v], out_sem.at[v])

    def pass_on(v):
        twin_copy(v).wait_recv()
        for k, row in ((1, 3 - near_y), (0, near_y)):
            sums[v, row, keep] += twin_part[v, row]
            side_copy(v, k).start()

    def finish(v):
        for k, row in ((1, far_y), (0, y)):
            side_copy(v, k).wait_recv()
            sums[v, row, keep] += twin_part[v, row] + side_part[v, k]
            if k == 1:
                out_copy(v, 1).start()
            else:

                @pl.when(home == 1)
                def _():
                    out_local(v).start()

                @pl.when(home == 0)
                def _():
                    out_copy(v, 0).start()

    def place(i):
        return i // 4, (i // 2) % 2, pl.ds(pl.multiple_of((i % 2) * 256, 256), 256)

    for copy in loads:
        copy.wait()

    mutual = (1 - home) * (4 + 8 * u)
    idle = (1 - home) * u

    def edge(t, _):
        past = (t + 15 - mutual) // 16
        now = (t + 16 - mutual) // 16 - past
        e = t - past
        from_4, from_6, from_7, from_9, from_10 = ((e + 16 - n) // 16 for n in (4, 6, 7, 9, 10))
        a = (1 - from_4) * (e // 2) + (from_4 - from_10) * ((e + 2) % 3) + from_10 * 2
        slot = (
            (1 - from_4) * (3 + e % 2) + (from_4 - from_6) * 5 + (from_6 - from_7) * 3
            + (from_7 - from_9) * 6 + from_9 * (e - 5)
        )
        itself = home * u * ((7 - slot) // 3 - (6 - slot) // 3)
        b = slot + itself * (a - slot)
        a = now * (1 - home) + (1 - now) * a
        b = now * (2 - home * u) + (1 - now) * b

        @pl.when((1 - home) * t == 2)
        def _():
            owned_in(1).wait_recv()

        @pl.when(t == 3 + home)
        def _():
            foreign_in(1).start()

        @pl.when(t == 4 + home)
        def _():
            @pl.when(home == 1)
            def _():
                foreign_wait(5)

            @pl.when(home == 0)
            def _():
                guest_load.wait()
                owned_in(2).wait_recv()

        @pl.when(e == 7)
        def _():
            foreign_wait(6)

        @pl.when(idle * t != 12)
        def _():
            forward(lambda rows: held[a, rows, :] * held[b, rows, :], table_z, table_r, first_ref)
            middle(kernel_ref, table_r, first_ref, second_ref)

            @pl.when(now == 0)
            def _():
                def emit(i, rows, value):
                    q, half, part = place(i)
                    sums[a, q, half, part, :] += held[b, rows, :] * value

                backward(emit, table_z, table_r, second_ref)

            @pl.when(now == 1)
            def _():
                def emit(i, rows, value):
                    q, half, part = place(i)
                    sums[a, q, half, part, :] += held[b, rows, :] * value
                    sums[b, q, half, part, :] += held[a, rows, :] * value

                backward(emit, table_z, table_r, second_ref)

        @pl.when(e == 7)
        def _():
            twin_copy(0).start()

        @pl.when(e == 8)
        def _():
            twin_copy(1).start()
            pass_on(0)

        @pl.when(e == 9)
        def _():
            pass_on(1)

        @pl.when(e == 11)
        def _():
            twin_copy(2).start()
            finish(0)

        return 0

    lax.fori_loop(0, 13, edge, 0)
    pass_on(2)
    finish(1)
    finish(2)

    for v in range(3):
        remote(sums.at[v, y, keep], out_ref.at[3 * (1 - h) + v], out_send.at[0], out_recv.at[3 * (1 - h) + v], flip_id).wait_recv()

    @pl.when(home == 0)
    def _():
        for v in range(3):
            remote(sums.at[v, y, keep], out_ref.at[3 * h + v], out_send.at[0], out_recv.at[3 * h + v], flip_id).wait_recv()
            out_copy(v, 0).wait_send()

    @pl.when(home == 1)
    def _():
        for v in range(3):
            owned_in(v).wait_send()
            out_local(v).wait()

    for v in range(3):
        foreign_in(v).wait_send()
        twin_copy(v).wait_send()
        side_copy(v, 0).wait_send()
        side_copy(v, 1).wait_send()
        out_copy(v, 1).wait_send()


def body(orbitals):
    flat = orbitals.reshape(6, ROWS, NZ)
    table_z, table_r = tables()
    anywhere = pl.BlockSpec(memory_space=pl.ANY)
    resident = pl.BlockSpec(memory_space=pltpu.VMEM)

    def buffer(*shape):
        return pltpu.VMEM(shape, f32)

    out = pl.pallas_call(
        fused_kernel,
        out_shape=jax.ShapeDtypeStruct((6, 512, NZ), f32),
        in_specs=[anywhere, anywhere, resident, resident],
        out_specs=anywhere,
        scratch_shapes=[
            buffer(7, ROWS, NZ),
            buffer(3, 4, 2, 512, NZ),
            buffer(ROWS, NZ),
            buffer(ROWS, NZ),
            buffer(ROWS, NZ),
            buffer(3, 4, 512, NZ),
            buffer(3, 2, 512, NZ),
        ]
        + [pltpu.SemaphoreType.DMA((count,)) for count in (7, 3, 3, 3, 4, 3, 3, 6, 6, 6, 6, 3)],
        compiler_params=pltpu.CompilerParams(
            vmem_limit_bytes=VMEM_LIMIT, collective_id=0, has_side_effects=True
        ),
        cost_estimate=pl.CostEstimate(flops=65 * 10**9, bytes_accessed=30 * 10**6, transcendentals=0),
    )(flat, screened_kernel(), table_z, table_r)
    return out.reshape(6, 8, NY, NZ)


def solution(mesh):
    return jax.shard_map(
        body,
        mesh=mesh,
        in_specs=(P("band", None, None, None),),
        out_specs=P("band", "pair", None, None),
        check_vma=False,
    )
```

```python
import math

import jax
import jax.numpy as jnp
import ml_dtypes
import numpy as np
from jax import lax
from jax.experimental import pallas as pl
from jax.experimental.pallas import tpu as pltpu
from jax.sharding import PartitionSpec as P

grid_spacing = 0.6
screening = 0.106

f32 = jnp.float32
bf16 = jnp.bfloat16
NX = 64
NY = 64
NZ = 128
ROWS = NX * NY
VMEM_LIMIT = 56 * 2**20
MESH = pl.DeviceIdType.MESH


def signed_freq(count):
    steps = np.arange(count)
    signed = np.where(steps <= count // 2, steps, steps - count)
    return signed * (2.0 * math.pi / (count * grid_spacing))


def screened_kernel():
    fx, fy, fz = signed_freq(NX), signed_freq(NY), signed_freq(NZ)
    square = fy[:, None, None] ** 2 + fx[None, :, None] ** 2 + fz[None, None, :] ** 2
    safe = np.where(square > 0, square, 1.0)
    value = 4.0 * math.pi / safe * -np.expm1(-safe / (4.0 * screening * screening))
    value = np.where(square > 0, value, math.pi / (screening * screening))
    value = (value * (-1.0 / (NX * NY * NZ))).astype(np.float32)
    return jnp.asarray(value.reshape(ROWS, NZ))


def cas(count):
    k = np.arange(count)
    angles = 2.0 * np.pi * ((k[:, None] * k[None, :]) % count) / count
    return np.cos(angles) + np.sin(angles)


def split_table(table):
    high = table.astype(ml_dtypes.bfloat16)
    low = (table - high.astype(np.float64)).astype(ml_dtypes.bfloat16)
    return high, low


def tables():
    high, low = split_table(cas(NZ))
    along_z = np.block([[high, low], [high, low]])
    high, low = split_table(cas(NY))
    zero = np.zeros_like(high)
    high = np.block([[high, zero], [zero, high]])
    low = np.block([[low, zero], [zero, low]])
    along_rows = np.block([[high, high], [low, low]])
    return jnp.asarray(along_z), jnp.asarray(along_rows)


def split(value):
    high = value.astype(bf16)
    low = (value - high.astype(f32)).astype(bf16)
    return high, low


def lanes_stage(value, table):
    high, low = split(value)
    out = jnp.dot(jnp.concatenate([high, low], axis=1), table, preferred_element_type=f32)
    return out[:, :NZ] + out[:, NZ:]


def rows_stage(tile, table):
    high, low = split(tile)
    out = jnp.dot(table, jnp.concatenate([high, low], axis=0), preferred_element_type=f32)
    return out[:128] + out[128:]


def to_tile(value):
    return jnp.concatenate([value[:128], value[128:]], axis=1)


def from_tile(tile):
    return jnp.concatenate([tile[:, :128], tile[:, 128:]], axis=0)


def store_turned(ref, group, value):
    turned = jnp.transpose(value.reshape(8, 8, 8, NZ), (1, 2, 0, 3))
    for high in range(8):
        for low in range(8):
            start = (high * 8 + low) * 64 + group * 8
            ref[pl.ds(pl.multiple_of(start, 8), 8), :] = turned[high, low]


def forward(load, table_z, table_r, first_ref):
    def step(i, _):
        rows = pl.ds(pl.multiple_of(i * 512, 512), 512)
        value = lanes_stage(load(rows), table_z)
        halves = [rows_stage(to_tile(value[:256]), table_r), rows_stage(to_tile(value[256:]), table_r)]
        store_turned(first_ref, i, jnp.concatenate([from_tile(tile) for tile in halves], axis=0))
        return 0

    lax.fori_loop(0, 8, step, 0, unroll=8)


def middle(kernel_ref, table_r, first_ref, second_ref):
    def step(i, _):
        halves = []
        for half in range(2):
            rows = pl.ds(pl.multiple_of(i * 512 + half * 256, 256), 256)
            tile = rows_stage(to_tile(first_ref[rows, :]), table_r)
            tile = tile * to_tile(kernel_ref[rows, :])
            halves.append(from_tile(rows_stage(tile, table_r)))
        store_turned(second_ref, i, jnp.concatenate(halves, axis=0))
        return 0

    lax.fori_loop(0, 8, step, 0, unroll=8)


def backward(emit, table_z, table_r, second_ref):
    def step(i, _):
        rows = pl.ds(pl.multiple_of(i * 256, 256), 256)
        tile = rows_stage(to_tile(second_ref[rows, :]), table_r)
        emit(i, rows, lanes_stage(from_tile(tile), table_z))
        return 0

    lax.fori_loop(0, 16, step, 0, unroll=16)


def fused_kernel(
    orb_ref, kernel_in, z_ref, r_ref, out_ref,
    held, sums, first_ref, second_ref, kernel_ref, twin_part, side_part,
    load_sem, owned_send, owned_recv, in_send, in_recv, twin_send, twin_recv, side_send, side_recv,
    out_send, out_recv, out_sem,
):
    band, pair = lax.axis_index("band"), lax.axis_index("pair")
    y, h = pair // 2, pair % 2
    core = band % 2
    side, u = y // 2, y % 2
    home = core * side + (1 - core) * (1 - side)
    twin = band + 1 - 2 * core
    block = band - core + side
    keep = home * h + (1 - home) * (1 - h)
    near_y = y + 1 - 2 * u
    far_y = 3 - y
    twin_id = (twin, pair)
    side_id = (band, near_y * 2 + h)
    across_id = (band, far_y * 2 + h)
    flip_id = (twin, y * 2 + 1 - h)
    corner_id = (twin, far_y * 2 + 1 - h)

    matched = core * (1 - side) + (1 - core) * side
    to_y = matched * y + (1 - matched) * far_y
    to_h = matched * h + (1 - matched) * (1 - h)
    forward_way = 2 * core - 1
    to_home = ((band + 16 + forward_way) % 16, to_y * 2 + to_h)
    to_guest = ((band + 16 + 2 * forward_way) % 16, to_y * 2 + to_h)
    foreign = (band - core + 15 + 3 * side) % 16
    from_same = (foreign, pair)
    from_other = (foreign, far_y * 2 + 1 - h)

    def load(source, slot):
        return pltpu.make_async_copy(orb_ref.at[source], held.at[slot], load_sem.at[slot])

    owned_loads = [load(3 * h + v, v) for v in range(3)]
    loads = [
        load(home * (3 * (1 - h) + 2 * u) + (1 - home) * 3 * u, 3),
        load(home * (3 * (1 - h) + 1) + (1 - home) * (3 * u + 1), 4),
    ]
    guest_load = load(3 * u + 2, 5)
    table_load = pltpu.make_async_copy(kernel_in, kernel_ref, load_sem.at[6])

    @pl.when(home == 1)
    def _():
        for copy in owned_loads:
            copy.start()

    table_load.start()
    for copy in loads:
        copy.start()

    @pl.when(home == 0)
    def _():
        guest_load.start()

    barrier = pltpu.get_barrier_semaphore()
    partners = (twin_id, side_id, across_id, flip_id, corner_id, to_home, to_guest, from_same, from_other)
    for other in partners:
        pl.semaphore_signal(barrier, inc=1, device_id=other, device_id_type=MESH)
    pl.semaphore_wait(barrier, len(partners))

    def remote(source, target_ref, send_sem, recv_sem, device):
        return pltpu.make_async_remote_copy(
            src_ref=source, dst_ref=target_ref, send_sem=send_sem, recv_sem=recv_sem,
            device_id=device, device_id_type=MESH,
        )

    def owned_in(v):
        return remote(orb_ref.at[3 * h + v], held.at[v], owned_send.at[v], owned_recv.at[v], twin_id)

    def foreign_in(j):
        slot = (5, 6, 6)[j]
        rows = pl.ds(pl.multiple_of((1 - matched) * 2048, 2048), 2048)
        source = orb_ref.at[3 * (to_y % 2) + j, rows, :]
        arrival = in_recv.at[(slot - 5) * 2 + 1 - matched]
        return remote(source, held.at[slot, rows, :], in_send.at[j], arrival, to_guest if j == 2 else to_home)

    def foreign_wait(slot):
        for half in range(2):
            rows = pl.ds(half * 2048, 2048)
            ref = held.at[slot, rows, :]
            remote(ref, ref, in_send.at[0], in_recv.at[(slot - 5) * 2 + half], from_same).wait_recv()

    @pl.when(home == 1)
    def _():
        for v in range(3):
            owned_in(v).start()

    for j in (0, 2):
        foreign_in(j).start()

    for v in range(3):
        sums[v] = jnp.zeros(sums.shape[1:], f32)
    table_z, table_r = z_ref[...], r_ref[...]

    @pl.when(home == 1)
    def _():
        for copy in owned_loads:
            copy.wait()

    @pl.when(home == 0)
    def _():
        owned_in(0).wait_recv()

    table_load.wait()

    slabs = (3 - near_y, near_y, far_y, y)

    def twin_copy(v, k):
        row, index = slabs[k], 4 * v + k
        source, target_ref = sums.at[v, row, 1 - keep], twin_part.at[v, row]
        return remote(source, target_ref, twin_send.at[index], twin_recv.at[index], twin_id)

    def twin_start(v):
        for k in range(4):
            twin_copy(v, k).start()

    def side_copy(v, k):
        row = (near_y, 3 - near_y)[k]
        index = 2 * v + k
        return remote(sums.at[v, row, keep], side_part.at[v, k], side_send.at[index], side_recv.at[index], side_id)

    def out_copy(v, k):
        row = (y, far_y)[k]
        return remote(
            sums.at[v, row, keep], out_ref.at[3 * h + v], out_send.at[2 * v + k], out_recv.at[3 * h + v],
            (block, row * 2 + keep),
        )

    def out_local(v):
        return pltpu.make_async_copy(sums.at[v, y, keep], out_ref.at[3 * h + v], out_sem.at[v])

    def pass_on(v):
        for k in range(2):
            twin_copy(v, k).wait_recv()
            sums[v, slabs[k], keep] += twin_part[v, slabs[k]]
            side_copy(v, 1 - k).start()

    def finish(v):
        for k, row in ((1, far_y), (0, y)):
            twin_copy(v, 3 - k).wait_recv()
            side_copy(v, k).wait_recv()
            sums[v, row, keep] += twin_part[v, row] + side_part[v, k]
            if k == 1:
                out_copy(v, 1).start()
            else:

                @pl.when(home == 1)
                def _():
                    out_local(v).start()

                @pl.when(home == 0)
                def _():
                    out_copy(v, 0).start()

    def place(i):
        return i // 4, (i // 2) % 2, pl.ds(pl.multiple_of((i % 2) * 256, 256), 256)

    for copy in loads:
        copy.wait()

    mutual = (1 - home) * (4 + 8 * u)
    idle = (1 - home) * u

    def edge(t, _):
        past = (t + 15 - mutual) // 16
        now = (t + 16 - mutual) // 16 - past
        e = t - past
        late, mid = e // 8, (e // 4) % 2
        a = late * 2 + (1 - late) * ((1 - mid) * ((e // 2) % 2) + mid * (e % 2))
        slot = 3 + late * (e % 4) + (1 - late) * ((1 - mid) * (e % 2) + mid * (2 + (e // 2) % 2))
        itself = home * u * ((7 - slot) // 3 - (6 - slot) // 3)
        b = slot + itself * (a - slot)
        a = now * (1 - home) + (1 - now) * a
        b = now * (2 - home * u) + (1 - now) * b

        @pl.when((1 - home) * t == 2)
        def _():
            owned_in(1).wait_recv()

        @pl.when(t == 3 + home)
        def _():
            foreign_in(1).start()

        @pl.when(t == 4 + home)
        def _():
            @pl.when(home == 1)
            def _():
                foreign_wait(5)

            @pl.when(home == 0)
            def _():
                guest_load.wait()
                owned_in(2).wait_recv()

        @pl.when(e == 6)
        def _():
            foreign_wait(6)

        @pl.when(idle * t != 12)
        def _():
            forward(lambda rows: held[a, rows, :] * held[b, rows, :], table_z, table_r, first_ref)
            middle(kernel_ref, table_r, first_ref, second_ref)

            @pl.when(e == 7)
            def _():
                pass_on(0)

            @pl.when(e == 8)
            def _():
                pass_on(1)

            @pl.when(now == 0)
            def _():
                def emit(i, rows, value):
                    q, half, part = place(i)
                    sums[a, q, half, part, :] += held[b, rows, :] * value

                backward(emit, table_z, table_r, second_ref)

            @pl.when(now == 1)
            def _():
                def emit(i, rows, value):
                    q, half, part = place(i)
                    sums[a, q, half, part, :] += held[b, rows, :] * value
                    sums[b, q, half, part, :] += held[a, rows, :] * value

                backward(emit, table_z, table_r, second_ref)

        @pl.when(e == 6)
        def _():
            twin_start(0)

        @pl.when(e == 7)
        def _():
            twin_start(1)

        @pl.when(e == 10)
        def _():
            finish(0)

        @pl.when(e == 11)
        def _():
            twin_start(2)

        return 0

    lax.fori_loop(0, 13, edge, 0)
    pass_on(2)
    finish(1)
    finish(2)

    for v in range(3):
        remote(sums.at[v, y, keep], out_ref.at[3 * (1 - h) + v], out_send.at[0], out_recv.at[3 * (1 - h) + v], flip_id).wait_recv()

    @pl.when(home == 0)
    def _():
        for v in range(3):
            remote(sums.at[v, y, keep], out_ref.at[3 * h + v], out_send.at[0], out_recv.at[3 * h + v], flip_id).wait_recv()
            out_copy(v, 0).wait_send()

    @pl.when(home == 1)
    def _():
        for v in range(3):
            owned_in(v).wait_send()
            out_local(v).wait()

    for v in range(3):
        foreign_in(v).wait_send()
        for k in range(4):
            twin_copy(v, k).wait_send()
        side_copy(v, 0).wait_send()
        side_copy(v, 1).wait_send()
        out_copy(v, 1).wait_send()


def body(orbitals):
    flat = orbitals.reshape(6, ROWS, NZ)
    table_z, table_r = tables()
    anywhere = pl.BlockSpec(memory_space=pl.ANY)
    resident = pl.BlockSpec(memory_space=pltpu.VMEM)

    def buffer(*shape):
        return pltpu.VMEM(shape, f32)

    out = pl.pallas_call(
        fused_kernel,
        out_shape=jax.ShapeDtypeStruct((6, 512, NZ), f32),
        in_specs=[anywhere, anywhere, resident, resident],
        out_specs=anywhere,
        scratch_shapes=[
            buffer(7, ROWS, NZ),
            buffer(3, 4, 2, 512, NZ),
            buffer(ROWS, NZ),
            buffer(ROWS, NZ),
            buffer(ROWS, NZ),
            buffer(3, 4, 512, NZ),
            buffer(3, 2, 512, NZ),
        ]
        + [pltpu.SemaphoreType.DMA((count,)) for count in (7, 3, 3, 3, 4, 12, 12, 6, 6, 6, 6, 3)],
        compiler_params=pltpu.CompilerParams(
            vmem_limit_bytes=VMEM_LIMIT, collective_id=0, has_side_effects=True
        ),
        cost_estimate=pl.CostEstimate(flops=65 * 10**9, bytes_accessed=30 * 10**6, transcendentals=0),
    )(flat, screened_kernel(), table_z, table_r)
    return out.reshape(6, 8, NY, NZ)


def solution(mesh):
    return jax.shard_map(
        body,
        mesh=mesh,
        in_specs=(P("band", None, None, None),),
        out_specs=P("band", "pair", None, None),
        check_vma=False,
    )
```

```python
import math

import jax
import jax.numpy as jnp
import ml_dtypes
import numpy as np
from jax import lax
from jax.experimental import pallas as pl
from jax.experimental.pallas import tpu as pltpu
from jax.sharding import PartitionSpec as P

grid_spacing = 0.6
screening = 0.106

f32 = jnp.float32
bf16 = jnp.bfloat16
NX = 64
NY = 64
NZ = 128
ROWS = NX * NY
VMEM_LIMIT = 56 * 2**20
MESH = pl.DeviceIdType.MESH


def signed_freq(count):
    steps = np.arange(count)
    signed = np.where(steps <= count // 2, steps, steps - count)
    return signed * (2.0 * math.pi / (count * grid_spacing))


def screened_kernel():
    fx, fy, fz = signed_freq(NX), signed_freq(NY), signed_freq(NZ)
    square = fy[:, None, None] ** 2 + fx[None, :, None] ** 2 + fz[None, None, :] ** 2
    safe = np.where(square > 0, square, 1.0)
    value = 4.0 * math.pi / safe * -np.expm1(-safe / (4.0 * screening * screening))
    value = np.where(square > 0, value, math.pi / (screening * screening))
    value = (value * (-1.0 / (NX * NY * NZ))).astype(np.float32)
    return jnp.asarray(value.reshape(ROWS, NZ))


def cas(count):
    k = np.arange(count)
    angles = 2.0 * np.pi * ((k[:, None] * k[None, :]) % count) / count
    return np.cos(angles) + np.sin(angles)


def split_table(table):
    high = table.astype(ml_dtypes.bfloat16)
    low = (table - high.astype(np.float64)).astype(ml_dtypes.bfloat16)
    return high, low


def tables():
    high, low = split_table(cas(NZ))
    along_z = np.block([[high, low], [high, low]])
    high, low = split_table(cas(NY))
    zero = np.zeros_like(high)
    high = np.block([[high, zero], [zero, high]])
    low = np.block([[low, zero], [zero, low]])
    along_rows = np.block([[high, high], [low, low]])
    return jnp.asarray(along_z), jnp.asarray(along_rows)


def split(value):
    high = value.astype(bf16)
    low = (value - high.astype(f32)).astype(bf16)
    return high, low


def lanes_stage(value, table):
    high, low = split(value)
    out = jnp.dot(jnp.concatenate([high, low], axis=1), table, preferred_element_type=f32)
    return out[:, :NZ] + out[:, NZ:]


def rows_stage(tile, table):
    high, low = split(tile)
    out = jnp.dot(table, jnp.concatenate([high, low], axis=0), preferred_element_type=f32)
    return out[:128] + out[128:]


def to_tile(value):
    return jnp.concatenate([value[:128], value[128:]], axis=1)


def from_tile(tile):
    return jnp.concatenate([tile[:, :128], tile[:, 128:]], axis=0)


def store_turned(ref, group, value):
    turned = jnp.transpose(value.reshape(8, 8, 8, NZ), (1, 2, 0, 3))
    for high in range(8):
        for low in range(8):
            start = (high * 8 + low) * 64 + group * 8
            ref[pl.ds(pl.multiple_of(start, 8), 8), :] = turned[high, low]


def forward(load, table_z, table_r, first_ref):
    def step(i, _):
        rows = pl.ds(pl.multiple_of(i * 512, 512), 512)
        value = lanes_stage(load(rows), table_z)
        halves = [rows_stage(to_tile(value[:256]), table_r), rows_stage(to_tile(value[256:]), table_r)]
        store_turned(first_ref, i, jnp.concatenate([from_tile(tile) for tile in halves], axis=0))
        return 0

    lax.fori_loop(0, 8, step, 0, unroll=8)


def middle(kernel_ref, table_r, first_ref, second_ref):
    def step(i, _):
        halves = []
        for half in range(2):
            rows = pl.ds(pl.multiple_of(i * 512 + half * 256, 256), 256)
            tile = rows_stage(to_tile(first_ref[rows, :]), table_r)
            tile = tile * to_tile(kernel_ref[rows, :])
            halves.append(from_tile(rows_stage(tile, table_r)))
        store_turned(second_ref, i, jnp.concatenate(halves, axis=0))
        return 0

    lax.fori_loop(0, 8, step, 0, unroll=8)


def backward(emit, table_z, table_r, second_ref):
    def step(i, _):
        rows = pl.ds(pl.multiple_of(i * 256, 256), 256)
        tile = rows_stage(to_tile(second_ref[rows, :]), table_r)
        emit(i, rows, lanes_stage(from_tile(tile), table_z))
        return 0

    lax.fori_loop(0, 16, step, 0, unroll=16)


def fused_kernel(
    orb_ref, kernel_in, z_ref, r_ref, out_ref,
    held, sums, first_ref, second_ref, kernel_ref, twin_part, side_part,
    load_sem, owned_send, owned_recv, in_send, in_recv, twin_send, twin_recv, side_send, side_recv,
    out_send, out_recv, out_sem,
):
    band, pair = lax.axis_index("band"), lax.axis_index("pair")
    y, h = pair // 2, pair % 2
    core = band % 2
    side, u = y // 2, y % 2
    home = core * side + (1 - core) * (1 - side)
    twin = band + 1 - 2 * core
    block = band - core + side
    keep = home * h + (1 - home) * (1 - h)
    near_y = y + 1 - 2 * u
    far_y = 3 - y
    twin_id = (twin, pair)
    side_id = (band, near_y * 2 + h)
    across_id = (band, far_y * 2 + h)
    flip_id = (twin, y * 2 + 1 - h)
    corner_id = (twin, far_y * 2 + 1 - h)

    matched = core * (1 - side) + (1 - core) * side
    to_y = matched * y + (1 - matched) * far_y
    to_h = matched * h + (1 - matched) * (1 - h)
    forward_way = 2 * core - 1
    to_home = ((band + 16 + forward_way) % 16, to_y * 2 + to_h)
    to_guest = ((band + 16 + 2 * forward_way) % 16, to_y * 2 + to_h)
    foreign = (band - core + 15 + 3 * side) % 16
    from_same = (foreign, pair)
    from_other = (foreign, far_y * 2 + 1 - h)

    def load(source, slot):
        return pltpu.make_async_copy(orb_ref.at[source], held.at[slot], load_sem.at[slot])

    owned_loads = [load(3 * h + v, v) for v in range(3)]
    loads = [
        load(home * (3 * (1 - h) + 2 * u) + (1 - home) * 3 * u, 3),
        load(home * (3 * (1 - h) + 1) + (1 - home) * (3 * u + 1), 4),
    ]
    guest_load = load(3 * u + 2, 5)
    table_load = pltpu.make_async_copy(kernel_in, kernel_ref, load_sem.at[6])

    @pl.when(home == 1)
    def _():
        for copy in owned_loads:
            copy.start()

    table_load.start()
    for copy in loads:
        copy.start()

    @pl.when(home == 0)
    def _():
        guest_load.start()

    barrier = pltpu.get_barrier_semaphore()
    partners = (twin_id, side_id, across_id, flip_id, corner_id, to_home, to_guest, from_same, from_other)
    for other in partners:
        pl.semaphore_signal(barrier, inc=1, device_id=other, device_id_type=MESH)
    pl.semaphore_wait(barrier, len(partners))

    def remote(source, target_ref, send_sem, recv_sem, device):
        return pltpu.make_async_remote_copy(
            src_ref=source, dst_ref=target_ref, send_sem=send_sem, recv_sem=recv_sem,
            device_id=device, device_id_type=MESH,
        )

    def owned_in(v):
        return remote(orb_ref.at[3 * h + v], held.at[v], owned_send.at[v], owned_recv.at[v], twin_id)

    def foreign_in(j):
        slot = (5, 6, 6)[j]
        rows = pl.ds(pl.multiple_of((1 - matched) * 2048, 2048), 2048)
        source = orb_ref.at[3 * (to_y % 2) + j, rows, :]
        arrival = in_recv.at[(slot - 5) * 2 + 1 - matched]
        return remote(source, held.at[slot, rows, :], in_send.at[j], arrival, to_guest if j == 2 else to_home)

    def foreign_wait(slot):
        for half in range(2):
            rows = pl.ds(half * 2048, 2048)
            ref = held.at[slot, rows, :]
            remote(ref, ref, in_send.at[0], in_recv.at[(slot - 5) * 2 + half], from_same).wait_recv()

    @pl.when(home == 1)
    def _():
        owned_in(0).start()

    for j in (0, 2):
        foreign_in(j).start()

    for v in range(3):
        sums[v] = jnp.zeros(sums.shape[1:], f32)
    table_z, table_r = z_ref[...], r_ref[...]

    @pl.when(home == 1)
    def _():
        for copy in owned_loads:
            copy.wait()

    @pl.when(home == 0)
    def _():
        owned_in(0).wait_recv()

    table_load.wait()

    slabs = (3 - near_y, near_y, far_y, y)

    def twin_copy(v, k):
        row, index = slabs[k], 4 * v + k
        source, target_ref = sums.at[v, row, 1 - keep], twin_part.at[v, row]
        return remote(source, target_ref, twin_send.at[index], twin_recv.at[index], twin_id)

    def twin_start(v):
        for k in range(4):
            twin_copy(v, k).start()

    def side_copy(v, k):
        row = (near_y, 3 - near_y)[k]
        index = 2 * v + k
        return remote(sums.at[v, row, keep], side_part.at[v, k], side_send.at[index], side_recv.at[index], side_id)

    def out_copy(v, k):
        row = (y, far_y)[k]
        return remote(
            sums.at[v, row, keep], out_ref.at[3 * h + v], out_send.at[2 * v + k], out_recv.at[3 * h + v],
            (block, row * 2 + keep),
        )

    def out_local(v):
        return pltpu.make_async_copy(sums.at[v, y, keep], out_ref.at[3 * h + v], out_sem.at[v])

    def pass_on(v):
        for k in range(2):
            twin_copy(v, k).wait_recv()
            sums[v, slabs[k], keep] += twin_part[v, slabs[k]]
            side_copy(v, 1 - k).start()

    def finish(v):
        for k, row in ((1, far_y), (0, y)):
            twin_copy(v, 3 - k).wait_recv()
            side_copy(v, k).wait_recv()
            sums[v, row, keep] += twin_part[v, row] + side_part[v, k]
            if k == 1:
                out_copy(v, 1).start()
            else:

                @pl.when(home == 1)
                def _():
                    out_local(v).start()

                @pl.when(home == 0)
                def _():
                    out_copy(v, 0).start()

    def place(i):
        return i // 4, (i // 2) % 2, pl.ds(pl.multiple_of((i % 2) * 256, 256), 256)

    for copy in loads:
        copy.wait()

    mutual = (1 - home) * (4 + 8 * u)
    idle = (1 - home) * u

    def edge(t, _):
        past = (t + 15 - mutual) // 16
        now = (t + 16 - mutual) // 16 - past
        e = t - past
        late, mid = e // 8, (e // 4) % 2
        a = late * 2 + (1 - late) * ((1 - mid) * ((e // 2) % 2) + mid * (e % 2))
        slot = 3 + late * (e % 4) + (1 - late) * ((1 - mid) * (e % 2) + mid * (2 + (e // 2) % 2))
        itself = home * u * ((7 - slot) // 3 - (6 - slot) // 3)
        b = slot + itself * (a - slot)
        a = now * (1 - home) + (1 - now) * a
        b = now * (2 - home * u) + (1 - now) * b

        @pl.when(home * t == 1)
        def _():
            owned_in(1).start()
            owned_in(2).start()

        @pl.when((1 - home) * t == 2)
        def _():
            owned_in(1).wait_recv()

        @pl.when(t == 3 + home)
        def _():
            foreign_in(1).start()

        @pl.when(t == 4 + home)
        def _():
            @pl.when(home == 1)
            def _():
                foreign_wait(5)

            @pl.when(home == 0)
            def _():
                guest_load.wait()
                owned_in(2).wait_recv()

        @pl.when(e == 6)
        def _():
            foreign_wait(6)

        @pl.when(idle * t != 12)
        def _():
            forward(lambda rows: held[a, rows, :] * held[b, rows, :], table_z, table_r, first_ref)
            middle(kernel_ref, table_r, first_ref, second_ref)

            @pl.when(e == 7)
            def _():
                pass_on(0)

            @pl.when(e == 8)
            def _():
                pass_on(1)

            @pl.when(now == 0)
            def _():
                def emit(i, rows, value):
                    q, half, part = place(i)
                    sums[a, q, half, part, :] += held[b, rows, :] * value

                backward(emit, table_z, table_r, second_ref)

            @pl.when(now == 1)
            def _():
                def emit(i, rows, value):
                    q, half, part = place(i)
                    sums[a, q, half, part, :] += held[b, rows, :] * value
                    sums[b, q, half, part, :] += held[a, rows, :] * value

                backward(emit, table_z, table_r, second_ref)

        @pl.when(e == 6)
        def _():
            twin_start(0)

        @pl.when(e == 7)
        def _():
            twin_start(1)

        @pl.when(e == 10)
        def _():
            finish(0)

        @pl.when(e == 11)
        def _():
            twin_start(2)

        return 0

    lax.fori_loop(0, 13, edge, 0)
    pass_on(2)
    finish(1)
    finish(2)

    for v in range(3):
        remote(sums.at[v, y, keep], out_ref.at[3 * (1 - h) + v], out_send.at[0], out_recv.at[3 * (1 - h) + v], flip_id).wait_recv()

    @pl.when(home == 0)
    def _():
        for v in range(3):
            remote(sums.at[v, y, keep], out_ref.at[3 * h + v], out_send.at[0], out_recv.at[3 * h + v], flip_id).wait_recv()
            out_copy(v, 0).wait_send()

    @pl.when(home == 1)
    def _():
        for v in range(3):
            owned_in(v).wait_send()
            out_local(v).wait()

    for v in range(3):
        foreign_in(v).wait_send()
        for k in range(4):
            twin_copy(v, k).wait_send()
        side_copy(v, 0).wait_send()
        side_copy(v, 1).wait_send()
        out_copy(v, 1).wait_send()


def body(orbitals):
    flat = orbitals.reshape(6, ROWS, NZ)
    table_z, table_r = tables()
    anywhere = pl.BlockSpec(memory_space=pl.ANY)
    resident = pl.BlockSpec(memory_space=pltpu.VMEM)

    def buffer(*shape):
        return pltpu.VMEM(shape, f32)

    out = pl.pallas_call(
        fused_kernel,
        out_shape=jax.ShapeDtypeStruct((6, 512, NZ), f32),
        in_specs=[anywhere, anywhere, resident, resident],
        out_specs=anywhere,
        scratch_shapes=[
            buffer(7, ROWS, NZ),
            buffer(3, 4, 2, 512, NZ),
            buffer(ROWS, NZ),
            buffer(ROWS, NZ),
            buffer(ROWS, NZ),
            buffer(3, 4, 512, NZ),
            buffer(3, 2, 512, NZ),
        ]
        + [pltpu.SemaphoreType.DMA((count,)) for count in (7, 3, 3, 3, 4, 12, 12, 6, 6, 6, 6, 3)],
        compiler_params=pltpu.CompilerParams(
            vmem_limit_bytes=VMEM_LIMIT, collective_id=0, has_side_effects=True
        ),
        cost_estimate=pl.CostEstimate(flops=65 * 10**9, bytes_accessed=30 * 10**6, transcendentals=0),
    )(flat, screened_kernel(), table_z, table_r)
    return out.reshape(6, 8, NY, NZ)


def solution(mesh):
    return jax.shard_map(
        body,
        mesh=mesh,
        in_specs=(P("band", None, None, None),),
        out_specs=P("band", "pair", None, None),
        check_vma=False,
    )
```

```python
import math

import jax
import jax.numpy as jnp
import ml_dtypes
import numpy as np
from jax import lax
from jax.experimental import pallas as pl
from jax.experimental.pallas import tpu as pltpu
from jax.sharding import PartitionSpec as P

grid_spacing = 0.6
screening = 0.106

f32 = jnp.float32
bf16 = jnp.bfloat16
NX = 64
NY = 64
NZ = 128
ROWS = NX * NY
VMEM_LIMIT = 56 * 2**20
MESH = pl.DeviceIdType.MESH


def signed_freq(count):
    steps = np.arange(count)
    signed = np.where(steps <= count // 2, steps, steps - count)
    return signed * (2.0 * math.pi / (count * grid_spacing))


def screened_kernel():
    fx, fy, fz = signed_freq(NX), signed_freq(NY), signed_freq(NZ)
    square = fy[:, None, None] ** 2 + fx[None, :, None] ** 2 + fz[None, None, :] ** 2
    safe = np.where(square > 0, square, 1.0)
    value = 4.0 * math.pi / safe * -np.expm1(-safe / (4.0 * screening * screening))
    value = np.where(square > 0, value, math.pi / (screening * screening))
    value = (value * (-1.0 / (NX * NY * NZ))).astype(np.float32)
    return jnp.asarray(value.reshape(ROWS, NZ))


def cas(count):
    k = np.arange(count)
    angles = 2.0 * np.pi * ((k[:, None] * k[None, :]) % count) / count
    return np.cos(angles) + np.sin(angles)


def split_table(table):
    high = table.astype(ml_dtypes.bfloat16)
    low = (table - high.astype(np.float64)).astype(ml_dtypes.bfloat16)
    return high, low


def tables():
    high, low = split_table(cas(NZ))
    along_z = np.block([[high, low], [high, low]])
    high, low = split_table(cas(NY))
    zero = np.zeros_like(high)
    high = np.block([[high, zero], [zero, high]])
    low = np.block([[low, zero], [zero, low]])
    along_rows = np.block([[high, high], [low, low]])
    return jnp.asarray(along_z), jnp.asarray(along_rows)


def split(value):
    high = value.astype(bf16)
    low = (value - high.astype(f32)).astype(bf16)
    return high, low


def lanes_stage(value, table):
    high, low = split(value)
    out = jnp.dot(jnp.concatenate([high, low], axis=1), table, preferred_element_type=f32)
    return out[:, :NZ] + out[:, NZ:]


def rows_stage(tile, table):
    high, low = split(tile)
    out = jnp.dot(table, jnp.concatenate([high, low], axis=0), preferred_element_type=f32)
    return out[:128] + out[128:]


def to_tile(value):
    return jnp.concatenate([value[:128], value[128:]], axis=1)


def from_tile(tile):
    return jnp.concatenate([tile[:, :128], tile[:, 128:]], axis=0)


def store_turned(ref, group, value):
    turned = jnp.transpose(value.reshape(8, 8, 8, NZ), (1, 2, 0, 3))
    for high in range(8):
        for low in range(8):
            start = (high * 8 + low) * 64 + group * 8
            ref[pl.ds(pl.multiple_of(start, 8), 8), :] = turned[high, low]


def forward(load, table_z, table_r, first_ref):
    def step(i, _):
        rows = pl.ds(pl.multiple_of(i * 512, 512), 512)
        value = lanes_stage(load(rows), table_z)
        halves = [rows_stage(to_tile(value[:256]), table_r), rows_stage(to_tile(value[256:]), table_r)]
        store_turned(first_ref, i, jnp.concatenate([from_tile(tile) for tile in halves], axis=0))
        return 0

    lax.fori_loop(0, 8, step, 0, unroll=8)


def middle(kernel_ref, table_r, first_ref, second_ref):
    def step(i, _):
        halves = []
        for half in range(2):
            rows = pl.ds(pl.multiple_of(i * 512 + half * 256, 256), 256)
            tile = rows_stage(to_tile(first_ref[rows, :]), table_r)
            tile = tile * to_tile(kernel_ref[rows, :])
            halves.append(from_tile(rows_stage(tile, table_r)))
        store_turned(second_ref, i, jnp.concatenate(halves, axis=0))
        return 0

    lax.fori_loop(0, 8, step, 0, unroll=8)


def backward(emit, table_z, table_r, second_ref):
    def step(i, _):
        rows = pl.ds(pl.multiple_of(i * 256, 256), 256)
        tile = rows_stage(to_tile(second_ref[rows, :]), table_r)
        emit(i, rows, lanes_stage(from_tile(tile), table_z))
        return 0

    lax.fori_loop(0, 16, step, 0, unroll=16)


def fused_kernel(
    orb_ref, kernel_in, z_ref, r_ref, out_ref,
    held, sums, first_ref, second_ref, kernel_ref, twin_part, side_part,
    load_sem, owned_send, owned_recv, in_send, in_recv, twin_send, twin_recv, side_send, side_recv,
    out_send, out_recv, out_sem,
):
    band, pair = lax.axis_index("band"), lax.axis_index("pair")
    y, h = pair // 2, pair % 2
    core = band % 2
    side, u = y // 2, y % 2
    home = core * side + (1 - core) * (1 - side)
    twin = band + 1 - 2 * core
    block = band - core + side
    keep = home * h + (1 - home) * (1 - h)
    near_y = y + 1 - 2 * u
    far_y = 3 - y
    twin_id = (twin, pair)
    side_id = (band, near_y * 2 + h)
    across_id = (band, far_y * 2 + h)
    flip_id = (twin, y * 2 + 1 - h)
    corner_id = (twin, far_y * 2 + 1 - h)

    matched = core * (1 - side) + (1 - core) * side
    to_y = matched * y + (1 - matched) * far_y
    to_h = matched * h + (1 - matched) * (1 - h)
    forward_way = 2 * core - 1
    to_home = ((band + 16 + forward_way) % 16, to_y * 2 + to_h)
    to_guest = ((band + 16 + 2 * forward_way) % 16, to_y * 2 + to_h)
    foreign = (band - core + 15 + 3 * side) % 16
    from_same = (foreign, pair)
    from_other = (foreign, far_y * 2 + 1 - h)

    def load(source, slot):
        return pltpu.make_async_copy(orb_ref.at[source], held.at[slot], load_sem.at[slot])

    owned_loads = [load(3 * h + v, v) for v in range(3)]
    loads = [
        load(home * (3 * (1 - h) + 2 * u) + (1 - home) * 3 * u, 3),
        load(home * (3 * (1 - h) + 1) + (1 - home) * (3 * u + 1), 4),
    ]
    guest_load = load(3 * u + 2, 5)
    table_load = pltpu.make_async_copy(kernel_in, kernel_ref, load_sem.at[6])

    @pl.when(home == 1)
    def _():
        for copy in owned_loads:
            copy.start()

    table_load.start()
    for copy in loads:
        copy.start()

    @pl.when(home == 0)
    def _():
        guest_load.start()

    barrier = pltpu.get_barrier_semaphore()
    partners = (twin_id, side_id, across_id, flip_id, corner_id, to_home, to_guest, from_same, from_other)
    for other in partners:
        pl.semaphore_signal(barrier, inc=1, device_id=other, device_id_type=MESH)
    pl.semaphore_wait(barrier, len(partners))

    def remote(source, target_ref, send_sem, recv_sem, device):
        return pltpu.make_async_remote_copy(
            src_ref=source, dst_ref=target_ref, send_sem=send_sem, recv_sem=recv_sem,
            device_id=device, device_id_type=MESH,
        )

    def owned_in(v):
        return remote(orb_ref.at[3 * h + v], held.at[v], owned_send.at[v], owned_recv.at[v], twin_id)

    def foreign_in(j):
        slot = (5, 6, 6)[j]
        rows = pl.ds(pl.multiple_of((1 - matched) * 2048, 2048), 2048)
        source = orb_ref.at[3 * (to_y % 2) + j, rows, :]
        arrival = in_recv.at[(slot - 5) * 2 + 1 - matched]
        return remote(source, held.at[slot, rows, :], in_send.at[j], arrival, to_guest if j == 2 else to_home)

    def foreign_wait(slot):
        for half in range(2):
            rows = pl.ds(half * 2048, 2048)
            ref = held.at[slot, rows, :]
            remote(ref, ref, in_send.at[0], in_recv.at[(slot - 5) * 2 + half], from_same).wait_recv()

    @pl.when(home == 1)
    def _():
        owned_in(0).start()

    for j in (0, 2):
        foreign_in(j).start()

    for v in range(3):
        sums[v] = jnp.zeros(sums.shape[1:], f32)
    table_z, table_r = z_ref[...], r_ref[...]

    @pl.when(home == 1)
    def _():
        for copy in owned_loads:
            copy.wait()

    @pl.when(home == 0)
    def _():
        owned_in(0).wait_recv()

    table_load.wait()

    slabs = (3 - near_y, near_y, far_y, y)

    def twin_copy(v, k):
        row, index = slabs[k], 4 * v + k
        source, target_ref = sums.at[v, row, 1 - keep], twin_part.at[v, row]
        return remote(source, target_ref, twin_send.at[index], twin_recv.at[index], twin_id)

    def twin_start(v):
        for k in range(4):
            twin_copy(v, k).start()

    def side_copy(v, k):
        row = (near_y, 3 - near_y)[k]
        index = 2 * v + k
        return remote(sums.at[v, row, keep], side_part.at[v, k], side_send.at[index], side_recv.at[index], side_id)

    def out_copy(v, k):
        row = (y, far_y)[k]
        return remote(
            sums.at[v, row, keep], out_ref.at[3 * h + v], out_send.at[2 * v + k], out_recv.at[3 * h + v],
            (block, row * 2 + keep),
        )

    def out_local(v):
        return pltpu.make_async_copy(sums.at[v, y, keep], out_ref.at[3 * h + v], out_sem.at[v])

    def pass_on(v):
        for k in range(2):
            twin_copy(v, k).wait_recv()
            sums[v, slabs[k], keep] += twin_part[v, slabs[k]]
            side_copy(v, 1 - k).start()

    def finish(v):
        for k, row in ((1, far_y), (0, y)):
            twin_copy(v, 3 - k).wait_recv()
            side_copy(v, k).wait_recv()
            sums[v, row, keep] += twin_part[v, row] + side_part[v, k]
            if k == 1:
                out_copy(v, 1).start()
            else:

                @pl.when(home == 1)
                def _():
                    out_local(v).start()

                @pl.when(home == 0)
                def _():
                    out_copy(v, 0).start()

    def place(i):
        return i // 4, (i // 2) % 2, pl.ds(pl.multiple_of((i % 2) * 256, 256), 256)

    for copy in loads:
        copy.wait()

    mutual = (1 - home) * (4 + 8 * u)
    idle = (1 - home) * u

    def edge(t, _):
        past = (t + 15 - mutual) // 16
        now = (t + 16 - mutual) // 16 - past
        e = t - past
        late, mid = e // 8, (e // 4) % 2
        a = late * 2 + (1 - late) * ((1 - mid) * ((e // 2) % 2) + mid * (e % 2))
        slot = 3 + late * (e % 4) + (1 - late) * ((1 - mid) * (e % 2) + mid * (2 + (e // 2) % 2))
        itself = home * u * ((7 - slot) // 3 - (6 - slot) // 3)
        b = slot + itself * (a - slot)
        a = now * (1 - home) + (1 - now) * a
        b = now * (2 - home * u) + (1 - now) * b

        @pl.when(home * t == 1)
        def _():
            owned_in(1).start()
            owned_in(2).start()

        @pl.when((1 - home) * t == 2)
        def _():
            owned_in(1).wait_recv()

        @pl.when(t == 2 + home)
        def _():
            foreign_in(1).start()

        @pl.when(t == 4 + home)
        def _():
            @pl.when(home == 1)
            def _():
                foreign_wait(5)

            @pl.when(home == 0)
            def _():
                guest_load.wait()
                owned_in(2).wait_recv()

        @pl.when(e == 6)
        def _():
            foreign_wait(6)

        @pl.when(idle * t != 12)
        def _():
            forward(lambda rows: held[a, rows, :] * held[b, rows, :], table_z, table_r, first_ref)
            middle(kernel_ref, table_r, first_ref, second_ref)

            @pl.when(e == 7)
            def _():
                pass_on(0)

            @pl.when(e == 8)
            def _():
                pass_on(1)

            @pl.when(now == 0)
            def _():
                def emit(i, rows, value):
                    q, half, part = place(i)
                    sums[a, q, half, part, :] += held[b, rows, :] * value

                backward(emit, table_z, table_r, second_ref)

            @pl.when(now == 1)
            def _():
                def emit(i, rows, value):
                    q, half, part = place(i)
                    sums[a, q, half, part, :] += held[b, rows, :] * value
                    sums[b, q, half, part, :] += held[a, rows, :] * value

                backward(emit, table_z, table_r, second_ref)

        @pl.when(e == 6)
        def _():
            twin_start(0)

        @pl.when(e == 7)
        def _():
            twin_start(1)

        @pl.when(e == 10)
        def _():
            finish(0)

        @pl.when(e == 11)
        def _():
            twin_start(2)

        return 0

    lax.fori_loop(0, 13, edge, 0)
    pass_on(2)
    finish(1)
    finish(2)

    for v in range(3):
        remote(sums.at[v, y, keep], out_ref.at[3 * (1 - h) + v], out_send.at[0], out_recv.at[3 * (1 - h) + v], flip_id).wait_recv()

    @pl.when(home == 0)
    def _():
        for v in range(3):
            remote(sums.at[v, y, keep], out_ref.at[3 * h + v], out_send.at[0], out_recv.at[3 * h + v], flip_id).wait_recv()
            out_copy(v, 0).wait_send()

    @pl.when(home == 1)
    def _():
        for v in range(3):
            owned_in(v).wait_send()
            out_local(v).wait()

    for v in range(3):
        foreign_in(v).wait_send()
        for k in range(4):
            twin_copy(v, k).wait_send()
        side_copy(v, 0).wait_send()
        side_copy(v, 1).wait_send()
        out_copy(v, 1).wait_send()


def body(orbitals):
    flat = orbitals.reshape(6, ROWS, NZ)
    table_z, table_r = tables()
    anywhere = pl.BlockSpec(memory_space=pl.ANY)
    resident = pl.BlockSpec(memory_space=pltpu.VMEM)

    def buffer(*shape):
        return pltpu.VMEM(shape, f32)

    out = pl.pallas_call(
        fused_kernel,
        out_shape=jax.ShapeDtypeStruct((6, 512, NZ), f32),
        in_specs=[anywhere, anywhere, resident, resident],
        out_specs=anywhere,
        scratch_shapes=[
            buffer(7, ROWS, NZ),
            buffer(3, 4, 2, 512, NZ),
            buffer(ROWS, NZ),
            buffer(ROWS, NZ),
            buffer(ROWS, NZ),
            buffer(3, 4, 512, NZ),
            buffer(3, 2, 512, NZ),
        ]
        + [pltpu.SemaphoreType.DMA((count,)) for count in (7, 3, 3, 3, 4, 12, 12, 6, 6, 6, 6, 3)],
        compiler_params=pltpu.CompilerParams(
            vmem_limit_bytes=VMEM_LIMIT, collective_id=0, has_side_effects=True
        ),
        cost_estimate=pl.CostEstimate(flops=65 * 10**9, bytes_accessed=30 * 10**6, transcendentals=0),
    )(flat, screened_kernel(), table_z, table_r)
    return out.reshape(6, 8, NY, NZ)


def solution(mesh):
    return jax.shard_map(
        body,
        mesh=mesh,
        in_specs=(P("band", None, None, None),),
        out_specs=P("band", "pair", None, None),
        check_vma=False,
    )
```

```python
import math

import jax
import jax.numpy as jnp
import ml_dtypes
import numpy as np
from jax import lax
from jax.experimental import pallas as pl
from jax.experimental.pallas import tpu as pltpu
from jax.sharding import PartitionSpec as P

grid_spacing = 0.6
screening = 0.106

f32 = jnp.float32
bf16 = jnp.bfloat16
NX = 64
NY = 64
NZ = 128
ROWS = NX * NY
VMEM_LIMIT = 56 * 2**20
MESH = pl.DeviceIdType.MESH


def signed_freq(count):
    steps = np.arange(count)
    signed = np.where(steps <= count // 2, steps, steps - count)
    return signed * (2.0 * math.pi / (count * grid_spacing))


def screened_kernel():
    fx, fy, fz = signed_freq(NX), signed_freq(NY), signed_freq(NZ)
    square = fy[:, None, None] ** 2 + fx[None, :, None] ** 2 + fz[None, None, :] ** 2
    safe = np.where(square > 0, square, 1.0)
    value = 4.0 * math.pi / safe * -np.expm1(-safe / (4.0 * screening * screening))
    value = np.where(square > 0, value, math.pi / (screening * screening))
    value = (value * (-1.0 / (NX * NY * NZ))).astype(np.float32)
    return jnp.asarray(value.reshape(ROWS, NZ))


def cas(count):
    k = np.arange(count)
    angles = 2.0 * np.pi * ((k[:, None] * k[None, :]) % count) / count
    return np.cos(angles) + np.sin(angles)


def split_table(table):
    high = table.astype(ml_dtypes.bfloat16)
    low = (table - high.astype(np.float64)).astype(ml_dtypes.bfloat16)
    return high, low


def tables():
    high, low = split_table(cas(NZ))
    along_z = np.block([[high, low], [high, low]])
    high, low = split_table(cas(NY))
    zero = np.zeros_like(high)
    high = np.block([[high, zero], [zero, high]])
    low = np.block([[low, zero], [zero, low]])
    along_rows = np.block([[high, high], [low, low]])
    return jnp.asarray(along_z), jnp.asarray(along_rows)


def split(value):
    high = value.astype(bf16)
    low = (value - high.astype(f32)).astype(bf16)
    return high, low


def lanes_stage(value, table):
    high, low = split(value)
    out = jnp.dot(jnp.concatenate([high, low], axis=1), table, preferred_element_type=f32)
    return out[:, :NZ] + out[:, NZ:]


def rows_stage(tile, table):
    high, low = split(tile)
    out = jnp.dot(table, jnp.concatenate([high, low], axis=0), preferred_element_type=f32)
    return out[:128] + out[128:]


def to_tile(value):
    return jnp.concatenate([value[:128], value[128:]], axis=1)


def from_tile(tile):
    return jnp.concatenate([tile[:, :128], tile[:, 128:]], axis=0)


def store_turned(ref, group, value):
    turned = jnp.transpose(value.reshape(8, 8, 8, NZ), (1, 2, 0, 3))
    for high in range(8):
        for low in range(8):
            start = (high * 8 + low) * 64 + group * 8
            ref[pl.ds(pl.multiple_of(start, 8), 8), :] = turned[high, low]


def forward(load, table_z, table_r, first_ref):
    def step(i, _):
        rows = pl.ds(pl.multiple_of(i * 512, 512), 512)
        value = lanes_stage(load(rows), table_z)
        halves = [rows_stage(to_tile(value[:256]), table_r), rows_stage(to_tile(value[256:]), table_r)]
        store_turned(first_ref, i, jnp.concatenate([from_tile(tile) for tile in halves], axis=0))
        return 0

    lax.fori_loop(0, 8, step, 0, unroll=8)


def middle(kernel_ref, table_r, first_ref, second_ref):
    def step(i, _):
        halves = []
        for half in range(2):
            rows = pl.ds(pl.multiple_of(i * 512 + half * 256, 256), 256)
            tile = rows_stage(to_tile(first_ref[rows, :]), table_r)
            tile = tile * to_tile(kernel_ref[rows, :])
            halves.append(from_tile(rows_stage(tile, table_r)))
        store_turned(second_ref, i, jnp.concatenate(halves, axis=0))
        return 0

    lax.fori_loop(0, 8, step, 0, unroll=8)


def backward(emit, table_z, table_r, second_ref):
    def step(i, _):
        rows = pl.ds(pl.multiple_of(i * 256, 256), 256)
        tile = rows_stage(to_tile(second_ref[rows, :]), table_r)
        emit(i, rows, lanes_stage(from_tile(tile), table_z))
        return 0

    lax.fori_loop(0, 16, step, 0, unroll=16)


def fused_kernel(
    orb_ref, kernel_in, z_ref, r_ref, out_ref,
    held, sums, first_ref, second_ref, kernel_ref, twin_part, side_part,
    load_sem, owned_send, owned_recv, in_send, in_recv, twin_send, twin_recv, side_send, side_recv,
    out_send, out_recv, out_sem,
):
    band, pair = lax.axis_index("band"), lax.axis_index("pair")
    y, h = pair // 2, pair % 2
    core = band % 2
    side, u = y // 2, y % 2
    home = core * side + (1 - core) * (1 - side)
    twin = band + 1 - 2 * core
    block = band - core + side
    keep = home * h + (1 - home) * (1 - h)
    near_y = y + 1 - 2 * u
    far_y = 3 - y
    twin_id = (twin, pair)
    side_id = (band, near_y * 2 + h)
    across_id = (band, far_y * 2 + h)
    flip_id = (twin, y * 2 + 1 - h)
    corner_id = (twin, far_y * 2 + 1 - h)

    matched = core * (1 - side) + (1 - core) * side
    to_y = matched * y + (1 - matched) * far_y
    to_h = matched * h + (1 - matched) * (1 - h)
    forward_way = 2 * core - 1
    to_home = ((band + 16 + forward_way) % 16, to_y * 2 + to_h)
    to_guest = ((band + 16 + 2 * forward_way) % 16, to_y * 2 + to_h)
    foreign = (band - core + 15 + 3 * side) % 16
    from_same = (foreign, pair)
    from_other = (foreign, far_y * 2 + 1 - h)

    def load(source, slot):
        return pltpu.make_async_copy(orb_ref.at[source], held.at[slot], load_sem.at[slot])

    owned_loads = [load(3 * h + v, v) for v in range(3)]
    loads = [
        load(home * (3 * (1 - h) + 2 * u) + (1 - home) * 3 * u, 3),
        load(home * (3 * (1 - h) + 1) + (1 - home) * (3 * u + 1), 4),
    ]
    guest_load = load(3 * u + 2, 5)
    table_load = pltpu.make_async_copy(kernel_in, kernel_ref, load_sem.at[6])

    @pl.when(home == 1)
    def _():
        for copy in owned_loads:
            copy.start()

    table_load.start()
    for copy in loads:
        copy.start()

    @pl.when(home == 0)
    def _():
        guest_load.start()

    barrier = pltpu.get_barrier_semaphore()
    partners = (twin_id, side_id, across_id, flip_id, corner_id, to_home, to_guest, from_same, from_other)
    for other in partners:
        pl.semaphore_signal(barrier, inc=1, device_id=other, device_id_type=MESH)
    pl.semaphore_wait(barrier, len(partners))

    def remote(source, target_ref, send_sem, recv_sem, device):
        return pltpu.make_async_remote_copy(
            src_ref=source, dst_ref=target_ref, send_sem=send_sem, recv_sem=recv_sem,
            device_id=device, device_id_type=MESH,
        )

    def owned_in(v):
        return remote(orb_ref.at[3 * h + v], held.at[v], owned_send.at[v], owned_recv.at[v], twin_id)

    def foreign_in(j):
        slot = (5, 6, 6)[j]
        rows = pl.ds(pl.multiple_of((1 - matched) * 2048, 2048), 2048)
        source = orb_ref.at[3 * (to_y % 2) + j, rows, :]
        arrival = in_recv.at[(slot - 5) * 2 + 1 - matched]
        return remote(source, held.at[slot, rows, :], in_send.at[j], arrival, to_guest if j == 2 else to_home)

    def foreign_wait(slot):
        for half in range(2):
            rows = pl.ds(half * 2048, 2048)
            ref = held.at[slot, rows, :]
            remote(ref, ref, in_send.at[0], in_recv.at[(slot - 5) * 2 + half], from_same).wait_recv()

    @pl.when(home == 1)
    def _():
        for v in range(3):
            owned_in(v).start()

    for j in (0, 2):
        foreign_in(j).start()

    for v in range(3):
        sums[v] = jnp.zeros(sums.shape[1:], f32)
    table_z, table_r = z_ref[...], r_ref[...]

    @pl.when(home == 1)
    def _():
        for copy in owned_loads:
            copy.wait()

    @pl.when(home == 0)
    def _():
        owned_in(0).wait_recv()

    table_load.wait()

    slabs = (3 - near_y, near_y, far_y, y)

    def twin_copy(v, k):
        row, index = slabs[k], 4 * v + k
        source, target_ref = sums.at[v, row, 1 - keep], twin_part.at[v, row]
        return remote(source, target_ref, twin_send.at[index], twin_recv.at[index], twin_id)

    def twin_start(v):
        for k in range(4):
            twin_copy(v, k).start()

    def side_copy(v, k):
        row = (near_y, 3 - near_y)[k]
        index = 2 * v + k
        return remote(sums.at[v, row, keep], side_part.at[v, k], side_send.at[index], side_recv.at[index], side_id)

    def out_copy(v, k):
        row = (y, far_y)[k]
        return remote(
            sums.at[v, row, keep], out_ref.at[3 * h + v], out_send.at[2 * v + k], out_recv.at[3 * h + v],
            (block, row * 2 + keep),
        )

    def out_local(v):
        return pltpu.make_async_copy(sums.at[v, y, keep], out_ref.at[3 * h + v], out_sem.at[v])

    def pass_on(v):
        for k in range(2):
            twin_copy(v, k).wait_recv()
            sums[v, slabs[k], keep] += twin_part[v, slabs[k]]
            side_copy(v, 1 - k).start()

    def finish(v):
        for k, row in ((1, far_y), (0, y)):
            twin_copy(v, 3 - k).wait_recv()
            side_copy(v, k).wait_recv()
            sums[v, row, keep] += twin_part[v, row] + side_part[v, k]
            if k == 1:
                out_copy(v, 1).start()
            else:

                @pl.when(home == 1)
                def _():
                    out_local(v).start()

                @pl.when(home == 0)
                def _():
                    out_copy(v, 0).start()

    def place(i):
        return i // 4, (i // 2) % 2, pl.ds(pl.multiple_of((i % 2) * 256, 256), 256)

    mutual = (1 - home) * (4 + 8 * u)
    idle = (1 - home) * u

    def edge(t, _):
        past = (t + 15 - mutual) // 16
        now = (t + 16 - mutual) // 16 - past
        e = t - past
        late, mid = e // 8, (e // 4) % 2
        a = late * 2 + (1 - late) * ((1 - mid) * ((e // 2) % 2) + mid * (e % 2))
        slot = 3 + late * (e % 4) + (1 - late) * ((1 - mid) * (e % 2) + mid * (2 + (e // 2) % 2))
        itself = home * u * ((7 - slot) // 3 - (6 - slot) // 3)
        b = slot + itself * (a - slot)
        a = now * (1 - home) + (1 - now) * a
        b = now * (2 - home * u) + (1 - now) * b

        @pl.when(t == home)
        def _():
            loads[0].wait()

        @pl.when(t == 1 + home)
        def _():
            loads[1].wait()

        @pl.when((1 - home) * t == 2)
        def _():
            owned_in(1).wait_recv()

        @pl.when(t == 3 + home)
        def _():
            foreign_in(1).start()

        @pl.when(t == 4 + home)
        def _():
            @pl.when(home == 1)
            def _():
                foreign_wait(5)

            @pl.when(home == 0)
            def _():
                guest_load.wait()
                owned_in(2).wait_recv()

        @pl.when(e == 6)
        def _():
            foreign_wait(6)

        @pl.when(idle * t != 12)
        def _():
            forward(lambda rows: held[a, rows, :] * held[b, rows, :], table_z, table_r, first_ref)
            middle(kernel_ref, table_r, first_ref, second_ref)

            @pl.when(e == 7)
            def _():
                pass_on(0)

            @pl.when(e == 8)
            def _():
                pass_on(1)

            @pl.when(now == 0)
            def _():
                def emit(i, rows, value):
                    q, half, part = place(i)
                    sums[a, q, half, part, :] += held[b, rows, :] * value

                backward(emit, table_z, table_r, second_ref)

            @pl.when(now == 1)
            def _():
                def emit(i, rows, value):
                    q, half, part = place(i)
                    sums[a, q, half, part, :] += held[b, rows, :] * value
                    sums[b, q, half, part, :] += held[a, rows, :] * value

                backward(emit, table_z, table_r, second_ref)

        @pl.when(e == 6)
        def _():
            twin_start(0)

        @pl.when(e == 7)
        def _():
            twin_start(1)

        @pl.when(e == 10)
        def _():
            finish(0)

        @pl.when(e == 11)
        def _():
            twin_start(2)

        return 0

    lax.fori_loop(0, 13, edge, 0)
    pass_on(2)
    finish(1)
    finish(2)

    for v in range(3):
        remote(sums.at[v, y, keep], out_ref.at[3 * (1 - h) + v], out_send.at[0], out_recv.at[3 * (1 - h) + v], flip_id).wait_recv()

    @pl.when(home == 0)
    def _():
        for v in range(3):
            remote(sums.at[v, y, keep], out_ref.at[3 * h + v], out_send.at[0], out_recv.at[3 * h + v], flip_id).wait_recv()
            out_copy(v, 0).wait_send()

    @pl.when(home == 1)
    def _():
        for v in range(3):
            owned_in(v).wait_send()
            out_local(v).wait()

    for v in range(3):
        foreign_in(v).wait_send()
        for k in range(4):
            twin_copy(v, k).wait_send()
        side_copy(v, 0).wait_send()
        side_copy(v, 1).wait_send()
        out_copy(v, 1).wait_send()


def body(orbitals):
    flat = orbitals.reshape(6, ROWS, NZ)
    table_z, table_r = tables()
    anywhere = pl.BlockSpec(memory_space=pl.ANY)
    resident = pl.BlockSpec(memory_space=pltpu.VMEM)

    def buffer(*shape):
        return pltpu.VMEM(shape, f32)

    out = pl.pallas_call(
        fused_kernel,
        out_shape=jax.ShapeDtypeStruct((6, 512, NZ), f32),
        in_specs=[anywhere, anywhere, resident, resident],
        out_specs=anywhere,
        scratch_shapes=[
            buffer(7, ROWS, NZ),
            buffer(3, 4, 2, 512, NZ),
            buffer(ROWS, NZ),
            buffer(ROWS, NZ),
            buffer(ROWS, NZ),
            buffer(3, 4, 512, NZ),
            buffer(3, 2, 512, NZ),
        ]
        + [pltpu.SemaphoreType.DMA((count,)) for count in (7, 3, 3, 3, 4, 12, 12, 6, 6, 6, 6, 3)],
        compiler_params=pltpu.CompilerParams(
            vmem_limit_bytes=VMEM_LIMIT, collective_id=0, has_side_effects=True
        ),
        cost_estimate=pl.CostEstimate(flops=65 * 10**9, bytes_accessed=30 * 10**6, transcendentals=0),
    )(flat, screened_kernel(), table_z, table_r)
    return out.reshape(6, 8, NY, NZ)


def solution(mesh):
    return jax.shard_map(
        body,
        mesh=mesh,
        in_specs=(P("band", None, None, None),),
        out_specs=P("band", "pair", None, None),
        check_vma=False,
    )
```
